32 devices in a mesh: dp: 8 (over y, x, core), tensor: 4 (over z).
Axes of the slice: x: 2, y: 2, z: 4, core: 2. Of those that a mesh axis runs over, the one named last changes fastest.
Arguments:
- block_input: bfloat16 [4096, 1536], P('dp'), may hold values from -6 to 6
- seq_lengths: int32 [2], replicated, may hold values from 1024 to 2048, as said below
- pre_gain: float32 [1536], replicated, may hold values from 0.5 to 1.5
- gate_weight: bfloat16 [1536, 3072], P(None, 'tensor'), may hold values from -0.15625 to 0.15625
- value_weight: bfloat16 [1536, 3072], P(None, 'tensor'), may hold values from -0.15625 to 0.15625
- state_proj: bfloat16 [1536, 256], replicated, may hold values from -0.15625 to 0.15625
- step_weight: bfloat16 [1536, 48], P(None, 'tensor'), may hold values from -0.15625 to 0.15625
- conv_weight: float32 [4, 3072], P(None, 'tensor'), may hold values from -3 to 3
- conv_bias: float32 [3072], P('tensor'), may hold values from -1.5 to 1.5
- state_conv_weight: float32 [4, 256], replicated, may hold values from -3 to 3
- state_conv_bias: float32 [256], replicated, may hold values from -1.5 to 1.5
- step_bias: float32 [48], P('tensor'), may hold values from -3 to 0
- decay_log: float32 [48], P('tensor'), may hold values from -8 to 0.5
- skip_gain: float32 [48], P('tensor'), may hold values from 0.5 to 1.5
- norm_gain: float32 [3072], P('tensor'), may hold values from 0.5 to 1.5
- out_weight: bfloat16 [3072, 1536], P('tensor'), may hold values from -0.109375 to 0.109375
- out_grad: bfloat16 [4096, 1536], P('dp'), may hold values from -6 to 6
Outputs:
- block_output: bfloat16 [4096, 1536], P('dp')
- input_grad: bfloat16 [4096, 1536], P('dp')
- pre_gain_grad: float32 [1536], P('dp')
- gate_weight_grad: float32 [1536, 3072], P('dp', 'tensor')
- value_weight_grad: float32 [1536, 3072], P('dp', 'tensor')
- state_proj_grad: float32 [1536, 256], P('dp')
- step_weight_grad: float32 [1536, 48], P('dp', 'tensor')
- conv_weight_grad: float32 [4, 3072], P(None, 'tensor')
- conv_bias_grad: float32 [3072], P('tensor')
- state_conv_weight_grad: float32 [4, 256], replicated
- state_conv_bias_grad: float32 [256], replicated
- step_bias_grad: float32 [48], P('tensor')
- decay_log_grad: float32 [48], P('tensor')
- skip_gain_grad: float32 [48], P('tensor')
- norm_gain_grad: float32 [3072], P('tensor')
- out_weight_grad: float32 [3072, 1536], P('tensor', 'dp')
The draws below stay inside these ranges and needn't reach their ends.
Inputs may be any that keep to these rules, and one draw needn't show every extreme that they name: `seq_lengths`: 2 lengths of the sequences packed one after another over all 4096 tokens, in order; they sum to 4096 and one of them is exactly 2048.
All inputs are finite; a program needn't handle non-finite values.
Results may differ from the reference program's by a relative error of at most 0.015.
Values may be sent and summed in bfloat16 or wider, within the bound.
A program may use at most 128 MiB of HBM per device.

```python
import jax
import jax.numpy as jnp
from jax import lax

D = 1536
HEADS = 48
HEADDIM = 64
STATE = 128
KCONV = 4
BLOCK = 256
MINLEN = 1024
MAXLEN = 2048
INNER = 3072
TOKENS = 4096
NSEQ = 2


def draw_seq_lengths(key, part):
    key = jax.random.fold_in(key, 11)
    loop_key = jax.random.fold_in(key, 1)
    order_key = jax.random.fold_in(key, 2)
    ceiling = MAXLEN - MINLEN
    others = NSEQ - 1
    remaining = TOKENS - NSEQ * MINLEN - ceiling
    divisor = max(others, 1)
    slots = jnp.arange(others, dtype=jnp.int32)
    extras = remaining // divisor + (slots < remaining % divisor).astype(jnp.int32)

    def transfer(step_index, current):
        step_key = jax.random.fold_in(loop_key, step_index)
        key_one, key_two, key_three = jax.random.split(step_key, 3)
        source = jax.random.randint(key_one, (), 0, divisor)
        target = jax.random.randint(key_two, (), 0, divisor)
        upper = jnp.minimum(current[source], ceiling - current[target]) + 1
        amount = jax.random.randint(key_three, (), 0, upper)
        return current.at[source].add(-amount).at[target].add(amount)
    extras = lax.fori_loop(0, 4 * others, transfer, extras)
    lengths_all = jnp.concatenate([jnp.full((1,), MAXLEN, jnp.int32), MINLEN + extras])
    order = jax.random.permutation(order_key, NSEQ)
    return lengths_all[order].astype(jnp.int32)


def draw_decay_log(key, part):
    key = jax.random.fold_in(key, 23)
    slow_key = jax.random.fold_in(key, 1)
    return jax.random.uniform(slow_key, (HEADS,), jnp.float32, -8.0, 0.5)


def block_scale(key, shape, cuts, least, largest):
    def one(axis_at, parts):
        heights = jax.random.uniform(jax.random.fold_in(jax.random.fold_in(key, 6), axis_at), (parts,), jnp.float32, least / len(cuts), largest / len(cuts))
        return jnp.repeat(jnp.exp(heights), shape[axis_at] // parts).reshape((-1,) + (1,) * (len(shape) - axis_at - 1))

    gain = one(*cuts[0])
    for cut in cuts[1:]:
        gain = gain * one(*cut)
    return gain


def scatter_about(rng, extent, scale, limit, cuts=(), held_as=jnp.bfloat16):
    level = block_scale(rng, extent, cuts, -0.22, 0.18) if cuts else 1.0
    drawn = jax.random.normal(rng, extent, jnp.float32) * scale * level
    return jnp.minimum(jnp.maximum(drawn, -limit), limit).astype(held_as)


def setup_inputs(seed: int = 0) -> dict:
    key_of = jax.random.split(jax.random.key(seed), 18)
    block_input = scatter_about(key_of[0], (TOKENS, D), 1.0, 6.0, ((0, 8),))
    seq_lengths = draw_seq_lengths(jax.random.fold_in(key_of[17], 71), 0)
    pre_gain = jnp.clip(1.0 + 0.1 * jax.random.normal(key_of[2], (D,), jnp.float32), 0.5, 1.5)
    gate_weight = scatter_about(key_of[3], (D, INNER), D ** -0.5, 0.15625, ((1, 4),))
    value_weight = scatter_about(key_of[4], (D, INNER), D ** -0.5, 0.15625, ((1, 4),))
    state_proj = scatter_about(key_of[5], (D, 2 * STATE), D ** -0.5, 0.15625)
    step_weight = scatter_about(key_of[6], (D, HEADS), D ** -0.5, 0.15625, ((1, 4),))
    conv_weight = scatter_about(key_of[7], (KCONV, INNER), 0.5, 3.0, ((1, 4),), jnp.float32)
    conv_bias = scatter_about(key_of[8], (INNER,), 0.3, 1.5, ((0, 4),), jnp.float32)
    state_conv_weight = scatter_about(key_of[9], (KCONV, 2 * STATE), 0.5, 3.0, (), jnp.float32)
    state_conv_bias = scatter_about(key_of[10], (2 * STATE,), 0.3, 1.5, (), jnp.float32)
    step_bias = jnp.clip(-3.0 + 3.0 * jax.random.uniform(key_of[11], (HEADS,), jnp.float32) ** block_scale(key_of[11], (HEADS,), ((0, 4),), -0.2, 0.2), -3.0, 0.0)
    decay_log = draw_decay_log(jax.random.fold_in(key_of[17], 71), 0)
    skip_gain = jnp.clip(0.5 + 1.0 * jax.random.uniform(key_of[13], (HEADS,), jnp.float32) ** block_scale(key_of[13], (HEADS,), ((0, 4),), -0.2, 0.2), 0.5, 1.5)
    norm_gain = jnp.clip(1.0 + 0.1 * jax.random.normal(key_of[14], (INNER,), jnp.float32), 0.5, 1.5)
    out_weight = scatter_about(key_of[15], (INNER, D), INNER ** -0.5, 0.109375, ((0, 4),))
    out_grad = scatter_about(key_of[16], (TOKENS, D), 1.0, 6.0, ((0, 8),))
    return dict(block_input=block_input, seq_lengths=seq_lengths, pre_gain=pre_gain, gate_weight=gate_weight, value_weight=value_weight, state_proj=state_proj, step_weight=step_weight, conv_weight=conv_weight, conv_bias=conv_bias, state_conv_weight=state_conv_weight, state_conv_bias=state_conv_bias, step_bias=step_bias, decay_log=decay_log, skip_gain=skip_gain, norm_gain=norm_gain, out_weight=out_weight, out_grad=out_grad)


epsilon = 1e-05
highest = lax.Precision.HIGHEST

@jax.custom_vjp
def low(v):
    return lax.optimization_barrier(v.astype(jnp.bfloat16)).astype(jnp.float32)

@jax.custom_vjp
def low_back(v):
    return v

def low_keep(v):
    return (low(v), None)

def low_pass(kept, grad):
    return (grad,)

def back_keep(v):
    return (v, None)

def back_low(kept, grad):
    return (low(grad),)
low.defvjp(low_keep, low_pass)
low_back.defvjp(back_keep, back_low)

def positions(seq_lengths, first_token, tok_count):
    tokens_at = first_token + jnp.arange(tok_count, dtype=jnp.int32)
    starts = jnp.cumsum(seq_lengths).astype(jnp.int32) - seq_lengths
    before = starts[None, :] <= tokens_at[:, None]
    seq_ids = lax.optimization_barrier(jnp.sum(before.astype(jnp.int32), axis=1)) - 1
    seq_start = lax.optimization_barrier(jnp.max(jnp.where(before, starts[None, :], 0), axis=1))
    return (seq_ids, tokens_at - seq_start)

def conv_apply(extended, weight, offset, seq_place, tok_count):
    tap_count = weight.shape[0]
    running_sum = jnp.zeros((tok_count, weight.shape[1]), extended.dtype) + offset
    for tap_index in range(tap_count):
        valid_tap = (seq_place >= tap_count - 1 - tap_index).astype(extended.dtype)[:, None]
        running_sum = running_sum + weight[tap_index] * extended[tap_index:tap_index + tok_count] * valid_tap
    return running_sum

def block_step(carry_state, pieces):
    values, step_sizes, logdec, input_mat, output_mat, seq_ids, resets = pieces
    block_len = values.shape[0]
    cum_log = jnp.cumsum(logdec, axis=0)
    causal = jnp.arange(block_len)[:, None] >= jnp.arange(block_len)[None, :]
    same_seq = ((seq_ids[:, None] == seq_ids[None, :]) & causal)[:, :, None]
    log_gap = cum_log[:, None, :] - cum_log[None, :, :]
    decay_mask = jnp.where(same_seq, jnp.exp(jnp.where(same_seq, log_gap, 0.0)), 0.0)
    scores = jnp.einsum('tn,sn->ts', output_mat, input_mat, precision=highest)
    mixed_scores = decay_mask * scores[:, :, None]
    weighted = values * step_sizes[:, :, None]
    within_block = jnp.einsum('tsh,shp->thp', mixed_scores, weighted, precision=highest)
    keep_mask = jnp.cumprod(1.0 - resets)
    carried = keep_mask[:, None] * jnp.exp(cum_log)
    carried_term = carried[:, :, None] * jnp.einsum('hpn,tn->thp', carry_state, output_mat, precision=highest)
    last_same = (seq_ids == seq_ids[-1]).astype(values.dtype)
    tail_weight = last_same[:, None] * jnp.exp(cum_log[-1][None, :] - cum_log)
    block_end = jnp.einsum('shp,sn->hpn', tail_weight[:, :, None] * weighted, input_mat, precision=highest)
    new_state = carried[-1][:, None, None] * carry_state + block_end
    return (new_state, within_block + carried_term)

def forward(block_input, pre_gain, gate_weight, value_weight, state_proj, step_weight, conv_weight, conv_bias, state_conv_weight, state_conv_bias, step_bias, decay_log, skip_gain, norm_gain, out_weight, seq_ids, seq_place, resets):
    inv_in = lax.rsqrt(lax.optimization_barrier(jnp.mean(block_input * block_input, axis=1, keepdims=True)) + epsilon)
    normed_in = low(block_input * inv_in * pre_gain)

    def project(weight):
        return low_back(low(jnp.dot(normed_in, weight, precision=highest)))
    gate_proj = project(gate_weight)
    values_raw = project(value_weight)
    state_raw = project(state_proj)
    step_raw = project(step_weight)
    pad_rows = KCONV - 1
    value_ext = jnp.concatenate([jnp.zeros((pad_rows, INNER), jnp.float32), values_raw], axis=0)
    state_ext = jnp.concatenate([jnp.zeros((pad_rows, 2 * STATE), jnp.float32), state_raw], axis=0)
    values = low(jax.nn.silu(conv_apply(value_ext, conv_weight, conv_bias, seq_place, TOKENS)))
    states = low(jax.nn.silu(conv_apply(state_ext, state_conv_weight, state_conv_bias, seq_place, TOKENS)))
    step_sizes = jax.nn.softplus(step_raw + step_bias)
    logdec = -jnp.exp(decay_log) * step_sizes
    block_total = TOKENS // BLOCK
    pieces = (values.reshape(block_total, BLOCK, HEADS, HEADDIM), step_sizes.reshape(block_total, BLOCK, HEADS), logdec.reshape(block_total, BLOCK, HEADS), states[:, :STATE].reshape(block_total, BLOCK, STATE), states[:, STATE:].reshape(block_total, BLOCK, STATE), seq_ids.reshape(block_total, BLOCK), resets.reshape(block_total, BLOCK))
    initial = jnp.zeros((HEADS, HEADDIM, STATE), jnp.float32)
    unused, scanned = lax.scan(jax.checkpoint(block_step), initial, pieces)
    mixer_out = scanned.reshape(TOKENS, HEADS, HEADDIM) + skip_gain[:, None] * values.reshape(TOKENS, HEADS, HEADDIM)
    mixer_out = mixer_out.reshape(TOKENS, INNER)
    gated_out = mixer_out * jax.nn.silu(gate_proj)
    inv_out = lax.rsqrt(lax.optimization_barrier(jnp.mean(gated_out * gated_out, axis=1, keepdims=True)) + epsilon)
    normed = low(gated_out * inv_out * norm_gain)
    return block_input + jnp.dot(normed, out_weight, precision=highest)

def reference(block_input, seq_lengths, pre_gain, gate_weight, value_weight, state_proj, step_weight, conv_weight, conv_bias, state_conv_weight, state_conv_bias, step_bias, decay_log, skip_gain, norm_gain, out_weight, out_grad):
    seq_ids, seq_place = positions(seq_lengths, 0, TOKENS)
    resets = (seq_place == 0).astype(jnp.float32)
    floats = tuple((element.astype(jnp.float32) for element in (block_input, pre_gain, gate_weight, value_weight, state_proj, step_weight, conv_weight, conv_bias, state_conv_weight, state_conv_bias, step_bias, decay_log, skip_gain, norm_gain, out_weight)))

    def wrapped(*params):
        return forward(*params, seq_ids, seq_place, resets)
    output, pullback = jax.vjp(wrapped, *floats)
    gradients = pullback(out_grad.astype(jnp.float32))
    return (output.astype(jnp.bfloat16), gradients[0].astype(jnp.bfloat16), gradients[1], gradients[2], gradients[3], gradients[4], gradients[5], gradients[6], gradients[7], gradients[8], gradients[9], gradients[10], gradients[11], gradients[12], gradients[13], gradients[14])
```

```python
import functools
import types

import jax
import jax.numpy as jnp
from jax import lax
from jax.experimental import pallas as pl
from jax.experimental.pallas import tpu as pltpu
from jax.sharding import PartitionSpec as P

F32 = jnp.float32
BF = jnp.bfloat16
MAXLEN = 2048
HEADDIM = 64
L = 128
RT = 32
LANES = 128
SUB = 256
HALO = 16
EPS = 1e-05
NEG = -1e30
VMEM_BYTES = 64 * 1024 * 1024 - 4096
DP = "dp"
TP = "tensor"


def mm(a, b):
    return lax.dot_general(a, b, (((1,), (0,)), ((), ())), preferred_element_type=F32)


def mm_rt(a, b):
    return lax.dot_general(a, b, (((1,), (1,)), ((), ())), preferred_element_type=F32)


def mm_lt(a, b):
    return lax.dot_general(a, b, (((0,), (0,)), ((), ())), preferred_element_type=F32)


def parts(a, n):
    out = []
    for _ in range(n - 1):
        hi = a.astype(BF)
        out.append(hi)
        a = a - hi.astype(F32)
    out.append(a.astype(BF))
    return out


def mm_fine(a, b, n=2):
    total = None
    for p in parts(a, n):
        t = mm(p, b)
        total = t if total is None else total + t
    return total


def mm_fine_right(a, b, n=3):
    total = None
    for p in parts(b, n):
        t = mm(a, p)
        total = t if total is None else total + t
    return total


def mm_rt_fine(a, b, n=3):
    total = None
    for p in parts(a, n):
        t = mm_rt(p, b)
        total = t if total is None else total + t
    return total


def wide(a, n):
    return jnp.concatenate([a] * n, axis=1) if n > 1 else a


def fold8(a):
    total = a[0:8]
    for i in range(8, a.shape[0], 8):
        total = total + a[i : i + 8]
    return total


def rows_loop(n, size, fn):
    def step(i, carry):
        fn(pl.multiple_of(i * size, size))
        return carry

    lax.fori_loop(0, n // size, step, 0)


def sigmoid(v):
    return 0.5 * jnp.tanh(0.5 * v) + 0.5


def silu_parts(v):
    sig = sigmoid(v)
    return v * sig, sig * (1.0 + v * (1.0 - sig))


class Plan:
    def __init__(self, mesh, x, lens, gw, sw, stepw, cw):
        self.dp = mesh.shape[DP]
        self.tp = mesh.shape[TP]
        self.tok, self.d = x.shape
        self.w = gw.shape[1]
        self.h = stepw.shape[0]
        self.s2 = sw.shape[1]
        self.ns = self.s2 // 2
        self.taps = cw.shape[0]
        self.nseq = lens.shape[0]
        self.total = self.tok * self.dp
        self.nb = self.tok // L
        self.pairs = self.h // 2
        self.nt = 256 if self.w % 256 == 0 else 128
        self.aligned = self.nseq * MAXLEN == self.total and MAXLEN % self.tok == 0
        self.group = MAXLEN // self.tok
        if self.aligned:
            self.reach = 1
        else:
            self.reach = min(-(-(MAXLEN - 1) // self.tok), self.dp - 1)
        self.srows = self.ns if self.aligned else self.ns + HALO
        self.nbits = self.dp.bit_length() - 1
        self.nc = self.d // LANES
        self.nsub = self.tok // SUB
        self.nch = self.nc * self.nsub
        self.cut = self.w // LANES // 2 * LANES
        self.crow = self.d // self.dp
        bits = list(range(self.nbits))
        self.order_a = bits
        self.order_b = bits[:1] + bits[1:][::-1]


def scratch_of(p):
    tok, d, w, ns, s2, nb, dp, tp = p.tok, p.d, p.w, p.ns, p.s2, p.nb, p.dp, p.tp
    v = lambda *s, t=BF: pltpu.VMEM(s, t)
    dma = lambda *s: pltpu.SemaphoreType.DMA(s)
    return dict(
        x=v(tok, d), gw=v(d, w), vw=v(d, w), sw=v(d, s2), ow=v(w, d), og=v(tok, d),
        in_sem=dma(6), pg=v(1, d, t=F32), cb=v(1, w, t=F32), ng=v(1, w, t=F32),
        swp=v(LANES, d), small=v(8, LANES, t=F32), E=v(LANES, w), ske=v(8, w, t=F32),
        hx=v(HALO, d), nx=v(tok + HALO, d), tb=v(d, tok), invin=v(tok, LANES, t=F32),
        vraw=v(tok + HALO, w), sraw=v(tok + HALO, s2), vgr=v(tok, w), sgr=v(tok, s2),
        val=v(tok, w), st=v(tok, s2), stT=v(s2, tok), gate=v(tok, w),
        sp=v(tok, LANES, t=F32), steps=v(tok, LANES, t=F32),
        cum=v(tok, LANES, t=F32), cumT=v(LANES, tok, t=F32),
        stepe=v(tok, w, t=F32), care=v(tok, w), taile=v(tok, w),
        facr=v(8 * nb, w, t=F32),
        wtd=v(tok, w), tw=v(tok, w), ends=v(nb, ns, w, t=F32), run=v(ns, w, t=F32),
        D=v(max(nb * p.pairs, p.nch), SUB, LANES), mixer=v(tok, w, t=F32), cp=v(tok, w), gn=v(tok, w),
        dn=v(tok + 8, w, t=F32), STb=v(nb, ns, w),
        sc=v(tok, LANES, t=F32),
        invo=v(tok, LANES, t=F32), coefo=v(tok, LANES, t=F32),
        dgate=v(tok, w), sdm=v(tok, w), rc=v(tok, LANES, t=F32),
        colT=v(LANES, L, t=F32), gsc=v(L, L, t=F32), rs=v(L, LANES, t=F32),
        gBC=v(tok, s2, t=F32), gf=v(8 * nb, w, t=F32), gtl=v(ns, w), dsp=v(tok + 8, s2, t=F32),
        dsl=v(tok, s2), dst=v(tok, LANES),
        acc=v(2, 8, w, t=F32), cacc=v(p.taps + 1, 8, max(w, s2), t=F32), pacc=v(8, d, t=F32),
        sacc=v(4, 8, LANES, t=F32),
        halo_sem=dma(6),
        fbuf=v(p.srows, w), fin=v(max(p.reach, 1), p.srows, w), fsem=dma(2, max(p.reach, 1)),
        bin=v(max(p.reach, 1), p.srows, w), bsem=dma(2, max(p.reach, 1)),
        zx=v(2, tp, 2 * nb, LANES, t=F32), zsem=dma(2, 2, tp),
        zs=v(tp, 8, d // 4, t=F32), zssem=dma(2, tp),
        sm=v(p.nbits + 1, 16, w, t=F32), sm_in=v(p.nbits, 16, w, t=F32), smsem=dma(2, p.nbits),
        Pf=v(p.nch, SUB, LANES), ar_a=v(2, p.nch, SUB, LANES), ar_b=v(p.nch, SUB, LANES),
        arsem=dma(2, 6, p.nch),
        w_gate=v(p.crow, w, t=F32), w_value=v(p.crow, w, t=F32), w_out=v(p.crow, w, t=F32), osem=dma(3),
        sq=v(p.crow, s2), sq_in=v(p.crow, s2), sq_x=v(p.crow, s2), sqsem=dma(5),
        g_out=v(dp, p.crow, w), r_out=v(dp - 1, p.crow, w), s_out=dma(2, dp),
        g_ss=v(dp, p.crow, s2 + LANES), g_gate=v(dp, p.crow, w), r_gate=v(dp - 1, p.crow, w), s_gate=dma(2, dp),
        r_va=v(dp - 1, p.crow, p.cut), s_va=dma(2, dp),
        r_vb=v(dp - 1, p.crow, w - p.cut), s_vb=dma(2, dp),
        r_ss=v(dp - 1, p.crow, s2 + LANES), s_ss=dma(2, dp),
    )


def kernel(p, names, few_in, few_out, *refs):
    r = types.SimpleNamespace(**dict(zip(names, refs)))
    by_name = dict(zip(names, refs))
    few_loads = [
        pltpu.make_async_copy(by_name[HBM + k], by_name[k], r.few_sem.at[0, i]) for i, k in enumerate(few_in)
    ]
    few_gives = [
        pltpu.make_async_copy(by_name[k], by_name[HBM + k], r.few_sem.at[1, i]) for i, k in enumerate(few_out)
    ]
    big = (r.x, r.gw, r.vw, r.sw, r.ow, r.og)
    sources = refs[: len(big)]
    tok, d, w, ns, s2, nb, dp, tp, pairs = p.tok, p.d, p.w, p.ns, p.s2, p.nb, p.dp, p.tp, p.pairs
    me = lax.axis_index(DP)
    rank = lax.axis_index(TP)
    first = me * tok
    wl = w // LANES
    inner = w * tp
    nt = p.nt

    def bit(v, b):
        return lax.rem(v // (2**b), 2)

    def remote(src, dst, ssem, rsem, axis, at):
        return pltpu.make_async_remote_copy(
            src_ref=src,
            dst_ref=dst,
            send_sem=ssem,
            recv_sem=rsem,
            device_id={axis: at},
            device_id_type=pl.DeviceIdType.MESH,
        )

    def load(at):
        return pltpu.make_async_copy(sources[at], big[at], r.in_sem.at[at])

    X, GW, VW, SW, OW, OG = range(len(big))
    load(X).start()
    for c in few_loads:
        c.start()
    for at in (VW, SW):
        load(at).start()

    barrier = pltpu.get_barrier_semaphore()
    for off in range(1, tp):
        pl.semaphore_signal(
            barrier, inc=1, device_id={TP: lax.rem(rank + off, tp)}, device_id_type=pl.DeviceIdType.MESH
        )
    for off in range(1, dp):
        pl.semaphore_signal(
            barrier, inc=1, device_id={DP: lax.rem(me + off, dp)}, device_id_type=pl.DeviceIdType.MESH
        )

    ahead = lax.rem(me, p.group)
    behind = p.group - 1 - ahead
    has_prev = ahead > 0 if p.aligned else me > 0
    has_next = behind > 0 if p.aligned else me < dp - 1
    starts = [jnp.int32(0)]
    for k in range(p.nseq - 1):
        starts.append(starts[-1] + r.lens[k])

    def start_of(g):
        at = jnp.zeros_like(g) if getattr(g, "shape", ()) else jnp.int32(0)
        for s in starts[1:]:
            at = jnp.where(g >= s, s, at)
        return at

    def place(t0, rows, width):
        g = first + t0 + lax.broadcasted_iota(jnp.int32, (rows, width), 0)
        return g - start_of(g)

    for c in few_loads:
        c.wait()
    row_w = lax.broadcasted_iota(jnp.int32, (LANES, w), 0)
    lane_w = lax.broadcasted_iota(jnp.int32, (LANES, w), 1)
    r.E[...] = jnp.where(lane_w // HEADDIM == row_w, 1.0, 0.0).astype(BF)
    r.small[...] = jnp.zeros((8, LANES), F32)
    r.small[0:1, 0 : p.h] = r.sb[...]
    r.small[1:2, 0 : p.h] = r.dl[...]
    r.small[2:3, 0 : p.h] = r.sk[...]
    r.ske[...] = mm_fine(jnp.broadcast_to(r.small[2:3, :], (8, LANES)), r.E[...], 3)
    r.swp[...] = jnp.zeros((LANES, d), BF)
    r.swp[0 : p.h, :] = r.stepw[...]
    r.pg[...] = r.pg_in[...].reshape(1, d)
    r.cb[...] = r.cb_in[...].reshape(1, w)
    r.ng[...] = r.ng_in[...].reshape(1, w)
    skip_row = r.ske[0:1, :]
    bias_row = r.small[0:1, :]
    decay_row = -jnp.exp(r.small[1:2, :])
    lane_l = lax.broadcasted_iota(jnp.int32, (L, LANES), 1)
    row_l = lax.broadcasted_iota(jnp.int32, (L, LANES), 0)

    load(X).wait()
    for at in (GW, OG, OW):
        load(at).start()
    pl.semaphore_wait(barrier, tp - 1 + dp - 1)

    def halo_copy():
        return remote(
            r.x.at[pl.ds(tok - HALO, HALO), :], r.hx, r.halo_sem.at[0], r.halo_sem.at[1],
            DP, jnp.minimum(me + 1, dp - 1),
        )

    @pl.when(has_next)
    def _():
        halo_copy().start()

    @pl.when(jnp.logical_not(has_prev))
    def _():
        r.hx[...] = jnp.zeros((HALO, d), BF)

    def ok_fwd(k, at):
        c = at >= k
        return jnp.logical_and(c, lax.rem(at, p.group) >= k) if p.aligned else c

    def ok_bwd(k, at):
        c = at + k < dp
        return jnp.logical_and(c, lax.rem(at, p.group) + k < p.group) if p.aligned else c

    def fwd_copy(k):
        return remote(
            r.fbuf, r.fin.at[k - 1], r.fsem.at[0, k - 1], r.fsem.at[1, k - 1], DP,
            jnp.minimum(me + k, dp - 1),
        )

    def bwd_copy(k):
        return remote(
            r.fbuf, r.bin.at[k - 1], r.bsem.at[0, k - 1], r.bsem.at[1, k - 1], DP,
            jnp.maximum(me - k, 0),
        )

    for k in range(1, p.reach + 1):

        @pl.when(jnp.logical_not(ok_fwd(k, me)))
        def _(k=k):
            r.fin[k - 1] = jnp.zeros((p.srows, w), BF)

        @pl.when(jnp.logical_not(ok_bwd(k, me)))
        def _(k=k):
            r.bin[k - 1] = jnp.zeros((p.srows, w), BF)

    def own_factor():
        f = r.facr[0:1, :]
        for c in range(1, nb):
            f = f * r.facr[8 * c : 8 * c + 1, :]
        return f


    def pass_on(copy, slots, first):
        f = own_factor()

        def body(t):
            rr = pl.ds(t, RT)
            state = r.run[rr, :]
            if not first:
                state = state + f * slots[0, rr, :].astype(F32)
            r.fbuf[rr, :] = state.astype(BF)

        rows_loop(ns, RT, body)
        copy(1).start()

    def send_states(copy, turn, has):
        if p.aligned:

            @pl.when(jnp.logical_and(turn == 0, turn < p.group - 1))
            def _():
                pass_on(copy, None, True)

            return

        def body(t):
            rr = pl.ds(t, RT)
            r.fbuf[rr, :] = r.run[rr, :].astype(BF)

        rows_loop(ns, RT, body)
        r.fbuf[ns : ns + HALO, :] = jnp.broadcast_to(own_factor(), (HALO, w)).astype(BF)
        for k in range(1, p.reach + 1):

            @pl.when(has(k))
            def _(k=k):
                copy(k).start()

    def relay_states(copy, slots, turn, lo, hi):
        if p.aligned:
            hi = min(hi, p.group - 1)
            if lo < hi:

                @pl.when(jnp.logical_and(turn >= lo, turn < hi))
                def _():
                    copy(1).wait_recv()
                    pass_on(copy, slots, False)

    def receive_states(copy, slots, turn, has):
        if p.aligned:

            @pl.when(jnp.logical_and(turn == p.group - 1, turn > 0))
            def _():
                copy(1).wait_recv()

            def body(t):
                rr = pl.ds(t, RT)
                r.run[rr, :] = slots[0, rr, :].astype(F32)

            rows_loop(ns, RT, body)
            return

        for k in range(1, p.reach + 1):

            @pl.when(has(k))
            def _(k=k):
                copy(k).wait_recv()

        def body(t):
            rr = pl.ds(t, RT)
            total = jnp.zeros((RT, w), F32)
            f = jnp.ones((1, w), F32)
            for k in range(p.reach):
                total = total + f * slots[k, rr, :].astype(F32)
                f = f * slots[k, ns : ns + HALO, :].astype(F32)[0:1]
            r.run[rr, :] = total

        rows_loop(ns, RT, body)

    def ar_sems(ph, kind, i):
        return r.arsem.at[ph, kind, i]

    def cols(i):
        return pl.ds(pl.multiple_of(i * LANES, LANES), LANES)

    nsub = p.nsub
    ar_src = (r.Pf, r.D)

    nch = p.nch

    def columns(i):
        return cols(i // nsub)

    def row0(i):
        return pl.multiple_of(lax.rem(i, nsub) * SUB, SUB) if isinstance(i, jax.Array) else i % nsub * SUB

    ar_dst = (r.o_block, r.o_input)

    half_t = tp // 2
    mid = jnp.logical_or(rank == half_t - 1, rank == half_t)
    inward = jnp.where(rank < half_t, rank + 1, rank - 1)
    outward = jnp.clip(jnp.where(rank < half_t, rank - 1, rank + 1), 0, tp - 1)
    end = jnp.logical_or(rank == 0, rank == tp - 1)
    ar_across = (r.ar_b, r.Pf)

    def ar_a(ph, i):
        return r.ar_a.at[ph, i]

    def ar_in(ph, i, src):
        return remote(src, ar_a(ph, i), ar_sems(ph, 0, i), ar_sems(ph, 1, i), TP, inward)

    def ar_swap(ph, i):
        return remote(
            ar_a(ph, i), ar_across[ph].at[i], ar_sems(ph, 0, i), ar_sems(ph, 2, i), TP, inward
        )

    def ar_out(ph, i, src):
        return remote(src, ar_a(ph, i), ar_sems(ph, 3, i), ar_sems(ph, 4, i), TP, outward)

    def ar_keep(ph, i, src):
        return pltpu.make_async_copy(src, ar_dst[ph].at[pl.ds(row0(i), SUB), columns(i)], ar_sems(ph, 5, i))

    def each_rows(i, fn):
        base = row0(i)
        rows_loop(SUB, L, lambda t: fn(pl.ds(t, L), pl.ds(pl.multiple_of(base + t, L), L)))

    def ar_start(ph, i):
        @pl.when(end)
        def _():
            ar_in(ph, i, ar_src[ph].at[i]).start()

    def ar_add(ph, i):
        @pl.when(end)
        def _():
            ar_in(ph, i, ar_a(ph, i)).wait_send()
            to, at = divmod(ph * nch + i + DEPTH, nch)
            if to < 2:
                ar_in(to, at, ar_src[to].at[at]).start()

        @pl.when(jnp.logical_not(end))
        def _():
            ar_in(ph, i, ar_a(ph, i)).wait_recv()

            def body(q, rr):
                r.ar_a[ph, i, q, :] = (r.ar_a[ph, i, q, :].astype(F32) + ar_src[ph][i, q, :].astype(F32)).astype(BF)

            each_rows(i, body)
            if half_t > 2:

                @pl.when(jnp.logical_not(mid))
                def _():
                    ar_in(ph, i, ar_a(ph, i)).start()

            @pl.when(mid)
            def _():
                ar_swap(ph, i).start()

    def ar_done(ph, i):
        @pl.when(mid)
        def _():
            ar_swap(ph, i).wait()
            got = ar_across[ph]

            def body(q, rr):
                total = r.ar_a[ph, i, q, :].astype(F32) + got[i, q, :].astype(F32)
                xt = r.x[rr, columns(i)].astype(F32)
                if ph == 0:
                    res = xt + total * r.invo[rr, :]
                else:
                    f = total * r.pg[0:1, columns(i)]
                    res = r.og[rr, columns(i)].astype(F32) + r.invin[rr, :] * f - xt * r.coefo[rr, :]
                got[i, q, :] = res.astype(BF)

            each_rows(i, body)
            ar_out(ph, i, got.at[i]).start()
            ar_keep(ph, i, got.at[i]).start()

        if half_t > 2:

            @pl.when(jnp.logical_not(jnp.logical_or(mid, end)))
            def _():
                here = ar_a(ph, i)
                ar_in(ph, i, here).wait_send()
                ar_out(ph, i, here).wait_recv()
                ar_out(ph, i, here).start()
                ar_keep(ph, i, here).start()

    def ar_finish(ph, i):
        here = ar_a(ph, i)

        @pl.when(end)
        def _():
            ar_out(ph, i, here).wait_recv()
            ar_keep(ph, i, here).start()

        @pl.when(jnp.logical_not(end))
        def _():
            ar_out(ph, i, here).wait_send()

    def ar_kept(ph, i):
        ar_keep(ph, i, ar_a(ph, i)).wait()

    LAG = 3
    DEPTH = 4
    FIN = LAG + 6
    KEPT = FIN + 4
    last_step = 2 * nch + LAG

    def ar_service(s0, s1):
        for s in range(s0, min(s1, last_step)):
            if s < 2 * nch:
                ar_add(*divmod(s, nch))
            if s >= LAG:
                ar_done(*divmod(s - LAG, nch))
            if s >= FIN:
                ar_finish(*divmod(s - FIN, nch))
            if s >= KEPT:
                ar_kept(*divmod(s - KEPT, nch))

    p_out = (r.g_out, 0, w, r.r_out, r.s_out, p.order_a)
    p_gate = (r.g_gate, 0, w, r.r_gate, r.s_gate, p.order_b)
    p_va = (r.g_out, 0, p.cut, r.r_va, r.s_va, p.order_a)
    p_vb = (r.g_out, p.cut, w, r.r_vb, r.s_vb, p.order_b)
    p_ss = (r.g_ss, 0, s2 + LANES, r.r_ss, r.s_ss, p.order_a)

    def rs_copy(piece, s, idx):
        g, lo, hi, got, sems, order = piece
        base = sum(dp // 2 ** (q + 1) for q in range(s))
        k = jnp.int32(0)
        for q in order[:s]:
            k = k + bit(me, q) * 2**q
        rem = [b for b in range(p.nbits) if b not in order[: s + 1]]
        for n, b in enumerate(rem):
            k = k + ((idx >> n) & 1) * 2**b
        b = order[s]
        mine = bit(me, b)
        keep = k + mine * 2**b
        send = k + (1 - mine) * 2**b
        src = g.at[send] if hi - lo == g.shape[2] else g.at[send, :, pl.ds(lo, hi - lo)]
        copy = remote(
            src, got.at[base + idx], sems.at[0, base + idx], sems.at[1, base + idx],
            DP, me + (1 - 2 * mine) * 2**b,
        )
        return copy, keep, base + idx

    def rs_send(piece, s):
        for idx in range(dp // 2 ** (s + 1)):
            rs_copy(piece, s, idx)[0].start()

    def rs_take(piece, s, out=None):
        g, lo, hi, got = piece[:4]
        last = s == p.nbits - 1
        for idx in range(dp // 2 ** (s + 1)):
            copy, keep, at = rs_copy(piece, s, idx)
            copy.wait_recv()

            def body(t, keep=keep, at=at):
                rr = pl.ds(t, RT)
                total = g[keep, rr, lo:hi].astype(F32) + got[at, rr, :].astype(F32)
                if last:
                    out(rr, total)
                else:
                    g[keep, rr, lo:hi] = total.astype(BF)

            rows_loop(p.crow, RT, body)
        if not last:
            rs_send(piece, s + 1)

    def rs_finish(piece):
        for s in range(p.nbits):
            for idx in range(dp // 2 ** (s + 1)):
                rs_copy(piece, s, idx)[0].wait_send()

    def zx_copy(which, off):
        return remote(
            r.zx.at[which, rank], r.zx.at[which, rank], r.zsem.at[which, 0, off], r.zsem.at[which, 1, off],
            TP, lax.rem(rank + off, tp),
        )

    def zx_send(which, src):
        for c in range(nb):
            turned = src[c * L : (c + 1) * L, :].T
            r.zx[which, rank, c : c + 1, :] = turned[0:1]
            r.zx[which, rank, nb + c : nb + c + 1, :] = turned[1:2]
        for off in range(1, tp):
            zx_copy(which, off).start()

    def zx_take(which, dst):
        for off in range(1, tp):
            zx_copy(which, off).wait_recv()
        total = r.zx[which, 0]
        for k in range(1, tp):
            total = total + r.zx[which, k]
        for c in range(nb):
            first = jnp.broadcast_to(total[c : c + 1], (LANES, L))
            second = jnp.broadcast_to(total[nb + c : nb + c + 1], (LANES, L))
            dst[c * L : (c + 1) * L, :] = jnp.where(row_l == 0, first, second).T

    def sm_copy(s):
        mine = bit(me, s)
        return remote(
            r.sm.at[s], r.sm_in.at[s], r.smsem.at[0, s], r.smsem.at[1, s], DP, me + (1 - 2 * mine) * 2**s
        )

    def sm_take(s):
        sm_copy(s).wait_recv()
        r.sm[s + 1] = r.sm[s] + r.sm_in[s]
        if s + 1 < p.nbits:
            sm_copy(s + 1).start()

    def slot_copy(buf, sems, axis, at, count, off):
        return remote(
            buf.at[at], buf.at[at], sems.at[0, off], sems.at[1, off], axis, lax.rem(at + off, count)
        )

    def norm_rows(src, s0, dst0, rows):
        xf = src[pl.ds(s0, rows), :].astype(F32)
        inv = lax.rsqrt(jnp.mean(xf * xf, axis=1, keepdims=True) + EPS)
        r.nx[pl.ds(dst0, rows), :] = (xf * inv * r.pg[...]).astype(BF)
        return inv

    def body(t):
        inv = norm_rows(r.x, t, pl.multiple_of(t + HALO, HALO), RT)
        r.invin[pl.ds(t, RT), :] = jnp.broadcast_to(inv, (RT, LANES))

    rows_loop(tok, RT, body)

    @pl.when(has_prev)
    def _():
        halo_copy().wait_recv()

    norm_rows(r.hx, 0, 0, HALO)
    load(VW).wait()
    load(SW).wait()

    def body(n):
        nn = pl.ds(n, nt)
        r.vraw[:, nn] = mm(r.nx[...], r.vw[:, nn]).astype(BF)

    rows_loop(w, nt, body)
    r.sraw[...] = mm(r.nx[...], r.sw[...]).astype(BF)
    r.sp[...] = mm_rt(r.nx[HALO : HALO + tok, :], r.swp[...]).astype(BF).astype(F32) + bias_row

    def conv(raw, cw, cb, width, val, grad):
        def body(t):
            win = raw[pl.ds(t, RT + HALO), :].astype(F32)
            at = None if p.aligned else place(t, RT, width)
            total = jnp.broadcast_to(cb[...], (RT, width))
            for k in range(p.taps):
                back = p.taps - 1 - k
                tap = win[HALO - back : HALO - back + RT]
                if back and not p.aligned:
                    tap = jnp.where(at >= back, tap, 0.0)
                total = total + cw[k : k + 1, :] * tap
            act, slope = silu_parts(total)
            val[pl.ds(t, RT), :] = act.astype(BF)
            grad[pl.ds(t, RT), :] = slope.astype(BF)

        rows_loop(tok, RT, body)

    conv(r.sraw, r.scw, r.scb, s2, r.st, r.sgr)
    conv(r.vraw, r.cw, r.cb, w, r.val, r.vgr)

    for c in range(nb):
        r.stT[:, c * L : (c + 1) * L] = r.st[c * L : (c + 1) * L, :].T

    tri = jnp.where(row_l >= lane_l, 1.0, 0.0).astype(BF)
    for c in range(nb):
        rr = slice(c * L, (c + 1) * L)
        b0 = first + c * L
        pre = r.sp[rr, :]
        steps = jnp.maximum(pre, 0.0) + jnp.log1p(jnp.exp(-jnp.abs(pre)))
        cum = mm_fine_right(tri, decay_row * steps, 3)
        r.steps[rr, :] = steps
        r.cum[rr, :] = cum
        r.cumT[:, rr] = cum.T
        car = jnp.exp(cum)
        tail = jnp.exp(cum[L - 1 : L, :] - cum)
        if not p.aligned:
            g = b0 + row_l
            car = jnp.where(start_of(g) < b0, car, 0.0)
            tail = jnp.where(g >= start_of(b0 + L - 1), tail, 0.0)
        r.invo[rr, :] = car
        r.coefo[rr, :] = tail
        last = mm_fine(car[L - 8 : L, :], r.E[...], 2)[7:8]
        r.facr[8 * c : 8 * c + 8, :] = jnp.broadcast_to(last, (8, w))

    def body(n):
        nn = pl.ds(n, nt)
        r.stepe[:, nn] = mm_fine(r.steps[...], r.E[:, nn], 2)
        r.care[:, nn] = mm(r.invo[...].astype(BF), r.E[:, nn]).astype(BF)
        r.taile[:, nn] = mm(r.coefo[...].astype(BF), r.E[:, nn]).astype(BF)

    rows_loop(w, nt, body)

    def body(t):
        rr = pl.ds(t, RT)
        weighted = r.val[rr, :].astype(F32) * r.stepe[rr, :]
        r.wtd[rr, :] = weighted.astype(BF)
        r.tw[rr, :] = (weighted * r.taile[rr, :].astype(F32)).astype(BF)

    rows_loop(tok, RT, body)

    r.run[...] = jnp.zeros((ns, w), F32)
    for c in range(nb):
        rr = slice(c * L, (c + 1) * L)
        r.ends[c] = mm(r.stT[0:ns, rr], r.tw[rr, :])
        f = r.facr[8 * c : 8 * c + 1, :]

        def body(t, c=c, f=f):
            q = pl.ds(t, RT)
            r.run[q, :] = r.ends[c, q, :] + f * r.run[q, :]

        rows_loop(ns, RT, body)
    send_states(fwd_copy, ahead, lambda k: ok_bwd(k, me))

    def in_block(c):
        rr = pl.ds(pl.multiple_of(c * L, L), L)
        b_rows = r.st[rr, 0:ns]
        c_rows = r.st[rr, ns:s2]
        return rr, b_rows, c_rows, mm_rt(c_rows, b_rows)

    def within(c, carry):
        rr, b_rows, c_rows, scores = in_block(c)
        gt = first + c * L + row_l
        gs = first + c * L + lane_l
        keep = gs <= gt
        if not p.aligned:
            keep = jnp.logical_and(keep, gs >= start_of(gt))
        bias = jnp.where(keep, 0.0, NEG)
        cum = r.cum[rr, :]
        cumt = r.cumT[:, rr]
        for pr in range(pairs):
            decays, mixes = [], []
            for h in (2 * pr, 2 * pr + 1):
                dec = jnp.exp(cum[:, h : h + 1] - cumt[h : h + 1, :] + bias)
                dec = dec.astype(BF)
                decays.append(dec)
                mixes.append((dec.astype(F32) * scores).astype(BF))
            r.D[c * pairs + pr] = jnp.concatenate(decays, axis=0)
            both = mm(jnp.concatenate(mixes, axis=0), r.wtd[rr, pr * LANES : (pr + 1) * LANES])
            r.mixer[rr, pr * LANES : (pr + 1) * LANES] = jnp.where(lane_l < HEADDIM, both[0:L], both[L:])
        return carry

    lax.fori_loop(0, 1, within, 0)
    relay_states(fwd_copy, r.fin, ahead, 1, 2)
    lax.fori_loop(1, nb, within, 0)

    load(GW).wait()

    def body(n):
        nn = pl.ds(n, nt)
        r.gate[:, nn] = mm(r.nx[HALO : HALO + tok, :], r.gw[:, nn]).astype(BF)

    rows_loop(w, nt, body)

    load(OG).wait()
    load(OW).wait()

    def body(n):
        nn = pl.ds(n, nt)
        r.dn[0:tok, nn] = mm_rt(r.og[...], r.ow[nn, :])

    rows_loop(w, nt, body)

    relay_states(fwd_copy, r.fin, ahead, 2, p.group)
    receive_states(fwd_copy, r.fin, ahead, lambda k: ok_fwd(k, me))
    for c in range(nb):
        rr = slice(c * L, (c + 1) * L)
        f = r.facr[8 * c : 8 * c + 1, :]

        def body(t, c=c, f=f):
            q = pl.ds(t, RT)
            now = r.run[q, :]
            hi, lo = parts(now, 2)
            r.STb[c, q, :] = hi
            r.gtl[q, :] = lo
            r.run[q, :] = r.ends[c, q, :] + f * now
            r.ends[c, q, :] = now

        rows_loop(ns, RT, body)
        proj = mm(r.st[rr, ns:s2], r.STb[c]) + mm(r.st[rr, ns:s2], r.gtl[...])
        proj = proj * r.care[rr, :].astype(F32)
        r.cp[rr, :] = proj.astype(BF)
        r.mixer[rr, :] = r.mixer[rr, :] + proj

    lane_t = lax.broadcasted_iota(jnp.int32, (RT, LANES), 1)

    def body(t):
        rr = pl.ds(t, RT)
        mixer = r.mixer[rr, :] + skip_row * r.val[rr, :].astype(F32)
        gate = r.gate[rr, :].astype(F32)
        gated = mixer * (gate * sigmoid(gate))
        gained = gated * r.ng[...]
        r.mixer[rr, :] = mixer
        r.gn[rr, :] = gained.astype(BF)
        squares = jnp.sum(gated * gated, axis=1, keepdims=True)
        cross = jnp.sum(r.dn[rr, :] * gained, axis=1, keepdims=True)
        r.sc[rr, :] = jnp.where(lane_t == 0, squares, jnp.where(lane_t == 1, cross, 0.0))

    rows_loop(tok, RT, body)
    zx_send(0, r.sc)

    def out_tile(n):
        nn = pl.ds(n, 256)
        full = mm(r.gn[...], r.ow[:, nn]).astype(BF)
        for half in range(2):
            for j in range(nsub):
                at = (n // LANES + half) * nsub + j
                r.Pf[at] = full[j * SUB : (j + 1) * SUB, half * LANES : (half + 1) * LANES]

    per_tile = 2 * nsub
    lead = -(-DEPTH // per_tile)
    for n in range(lead):
        out_tile(n * 256)
        for i in range(n * per_tile, min((n + 1) * per_tile, DEPTH)):
            ar_start(0, i)
    rows_loop(d - lead * 256, 256, lambda n: out_tile(pl.multiple_of(n + lead * 256, 256)))

    for c in range(nb):
        r.tb[:, c * L : (c + 1) * L] = r.og[c * L : (c + 1) * L, :].T

    zx_take(0, r.sc)

    def body(t):
        rr = pl.ds(t, L)
        inv = lax.rsqrt(r.sc[rr, 0:1] * (1.0 / inner) + EPS)
        r.invo[rr, :] = jnp.broadcast_to(inv, (L, LANES))
        r.coefo[rr, :] = jnp.broadcast_to(inv * inv * inv * r.sc[rr, 1:2] * (1.0 / inner), (L, LANES))

    rows_loop(tok, L, body)

    r.acc[...] = jnp.zeros((2, 8, w), F32)

    def body(t):
        rr = pl.ds(t, RT)
        mixer = r.mixer[rr, :]
        act, slope = silu_parts(r.gate[rr, :].astype(F32))
        gated = mixer * act
        inv = wide(r.invo[rr, :], wl)
        coef = wide(r.coefo[rr, :], wl)
        dn = r.dn[rr, :]
        scaled = gated * inv
        dgated = inv * (dn * r.ng[...]) - gated * coef
        dmix = dgated * act
        val = r.val[rr, :].astype(F32)
        r.dgate[rr, :] = (dgated * mixer * slope).astype(BF)
        r.gn[rr, :] = (scaled * r.ng[...]).astype(BF)
        r.gate[rr, :] = dmix.astype(BF)
        r.dn[rr, :] = dmix
        hi, lo = parts(dmix * r.care[rr, :].astype(F32), 2)
        r.sdm[rr, :] = hi
        r.care[rr, :] = lo
        r.cp[rr, :] = (dmix * r.cp[rr, :].astype(F32)).astype(BF)
        r.acc[0] = r.acc[0] + fold8(dn * scaled)
        r.acc[1] = r.acc[1] + fold8(dmix * val)

    rows_loop(tok, RT, body)

    r.run[...] = jnp.zeros((ns, w), F32)
    for c in range(nb - 1, -1, -1):
        rr = slice(c * L, (c + 1) * L)
        r.mixer[rr, :] = mm(r.stT[ns:s2, rr], r.sdm[rr, :]) + mm(r.stT[ns:s2, rr], r.care[rr, :])
        f = r.facr[8 * c : 8 * c + 1, :]

        def body(t, c=c, f=f):
            q = pl.ds(t, RT)
            r.run[q, :] = r.mixer[pl.ds(pl.multiple_of(c * L + t, RT), RT), :] + f * r.run[q, :]

        rows_loop(ns, RT, body)
    for k in range(1, p.reach + 1):

        @pl.when(ok_bwd(k, me))
        def _(k=k):
            fwd_copy(k).wait_send()

    send_states(bwd_copy, behind, lambda k: ok_fwd(k, me))

    for c in range(nb):
        rr = slice(c * L, (c + 1) * L)
        r.gtl[...] = (r.ends[c] - r.STb[c].astype(F32)).astype(BF)
        r.gBC[rr, ns:s2] = (
            mm_rt(r.sdm[rr, :], r.STb[c])
            + mm_rt(r.care[rr, :], r.STb[c])
            + mm_rt(r.sdm[rr, :], r.gtl[...])
        )
    r.rc[...] = mm_rt(r.cp[...], r.E[...])
    relay_states(bwd_copy, r.bin, behind, 1, 2)
    ar_service(0, 4)

    def weight_grad(lhs, rhs, into, width, step):
        def body(n):
            nn = pl.ds(n, step)
            full = mm(lhs[...], rhs[:, nn]).astype(BF)
            for k in range(dp):
                into[k, :, nn] = full[k * p.crow : (k + 1) * p.crow, :]

        rows_loop(width, step, body)

    weight_grad(r.tb, r.gn, r.g_out, w, nt)
    rs_send(p_out, 0)
    ar_service(4, 5)

    def transpose_nx():
        for c in range(nb):
            r.tb[:, c * L : (c + 1) * L] = r.nx[HALO + c * L : HALO + (c + 1) * L, :].T

    transpose_nx()
    weight_grad(r.tb, r.dgate, r.g_gate, w, nt)
    rs_send(p_gate, 0)
    ar_service(5, 7)
    rs_take(p_out, 0)

    def within_back(c, carry):
        rr, b_rows, c_rows, scores = in_block(c)
        two = jnp.concatenate([scores, scores], axis=0)
        r.gsc[...] = jnp.zeros((L, L), F32)
        r.rs[...] = r.rc[rr, :]
        r.colT[...] = jnp.zeros((LANES, L), F32)
        low = lane_l < HEADDIM
        for pr in range(pairs):
            pc = slice(pr * LANES, (pr + 1) * LANES)
            dm = r.gate[rr, pc]
            zero = jnp.zeros_like(dm)
            stacked = jnp.concatenate([jnp.where(low, dm, zero), jnp.where(low, zero, dm)], axis=0)
            fine = r.dn[rr, pc] - dm.astype(F32)
            fine = jnp.concatenate([jnp.where(low, fine, 0.0), jnp.where(low, 0.0, fine)], axis=0).astype(BF)
            gm = mm_rt(stacked, r.wtd[rr, pc]) + mm_rt(fine, r.wtd[rr, pc])
            dec = r.D[c * pairs + pr].astype(F32)
            xx = gm * dec
            r.gsc[...] = r.gsc[...] + (xx[0:L] + xx[L:])
            mix = (dec * two).astype(BF)
            gap = (xx * two).astype(BF)
            gapf = gap.astype(F32)
            total = r.rs[...]
            for half in (0, 1):
                h = 2 * pr + half
                hot = jnp.where(lane_l == h, 1.0, 0.0).astype(BF)
                total = total + mm(gap[half * L : (half + 1) * L], hot)
                r.colT[h : h + 1, :] = jnp.sum(gapf[half * L : (half + 1) * L], axis=0, keepdims=True)
            r.rs[...] = total
            r.dn[rr, pc] = mm_lt(mix, stacked)
        low_scores = r.gsc[...].astype(BF)
        r.gBC[rr, ns:s2] = r.gBC[rr, ns:s2] + mm(low_scores, b_rows)
        r.gBC[rr, 0:ns] = mm_lt(low_scores, c_rows)
        r.rc[rr, :] = r.rs[...] - r.colT[...].T
        return carry

    lax.fori_loop(0, nb // 2, within_back, 0)
    rs_take(p_gate, 0)
    ar_service(7, 8)
    lax.fori_loop(nb // 2, nb, within_back, 0)
    ar_service(8, 10)

    relay_states(bwd_copy, r.bin, behind, 2, p.group)
    receive_states(bwd_copy, r.bin, behind, lambda k: ok_bwd(k, me))
    for c in range(nb - 1, -1, -1):
        rr = slice(c * L, (c + 1) * L)
        f = r.facr[8 * c : 8 * c + 1, :]
        r.gf[8 * c : 8 * c + 8, :] = jnp.zeros((8, w), F32)

        def body(t, c=c, f=f):
            q = pl.ds(t, RT)
            now = r.run[q, :]
            gf = r.gf[8 * c : 8 * c + 8, :]
            r.gf[8 * c : 8 * c + 8, :] = gf + fold8(now * r.ends[c, q, :])
            hi, lo = parts(now, 2)
            r.gtl[q, :] = lo
            r.STb[c, q, :] = hi
            r.run[q, :] = r.mixer[pl.ds(pl.multiple_of(c * L + t, RT), RT), :] + f * now

        rows_loop(ns, RT, body)
        gf = jnp.sum(r.gf[8 * c : 8 * c + 8, :], axis=0, keepdims=True) * f
        r.gf[8 * c : 8 * c + 8, :] = jnp.broadcast_to(gf, (8, w))
        r.mixer[rr, :] = mm(r.st[rr, 0:ns], r.STb[c])
        r.gBC[rr, 0:ns] = r.gBC[rr, 0:ns] + (
            mm_rt(r.tw[rr, :], r.STb[c]) + mm_rt(r.tw[rr, :], r.gtl[...])
        )

    def body(t):
        rr = pl.ds(t, RT)
        thr = r.mixer[rr, :]
        gw_ = r.dn[rr, :] + r.taile[rr, :].astype(F32) * thr
        val = r.val[rr, :].astype(F32)
        dval = skip_row * r.gate[rr, :].astype(F32) + gw_ * r.stepe[rr, :]
        r.sdm[rr, :] = (gw_ * val).astype(BF)
        r.cp[rr, :] = (r.tw[rr, :].astype(F32) * thr).astype(BF)
        r.dn[rr, :] = dval * r.vgr[rr, :].astype(F32)
        r.dsp[rr, :] = r.gBC[rr, :] * r.sgr[rr, :].astype(F32)

    rows_loop(tok, RT, body)

    def back_copy(which):
        buf = r.dn if which == 0 else r.dsp
        return remote(
            buf.at[pl.ds(0, 8), :], buf.at[pl.ds(tok, 8), :], r.halo_sem.at[2 + which], r.halo_sem.at[4 + which],
            DP, jnp.maximum(me - 1, 0),
        )

    @pl.when(has_prev)
    def _():
        back_copy(0).start()
        back_copy(1).start()

    @pl.when(jnp.logical_not(has_next))
    def _():
        r.dn[tok : tok + 8, :] = jnp.zeros((8, w), F32)
        r.dsp[tok : tok + 8, :] = jnp.zeros((8, s2), F32)

    ar_service(10, 12)

    up = jnp.where(lane_l >= row_l, 1.0, 0.0).astype(BF)
    below = jnp.where(lane_l < row_l, 1.0, 0.0).astype(BF)
    r.sacc[...] = jnp.zeros((4, 8, LANES), F32)
    for c in range(nb):
        rr = slice(c * L, (c + 1) * L)
        direct = mm_rt(r.sdm[rr, :], r.E[...])
        tails = mm_rt(r.cp[rr, :], r.E[...])
        gf = mm_rt_fine(r.gf[8 * c : 8 * c + 8, :], r.E[...], 3)[0:1]
        q = mm_fine_right(up, r.rc[rr, :], 3) + mm_fine_right(below, tails, 3) + gf
        steps = r.steps[rr, :]
        dstep = decay_row * q + direct
        dpre = dstep * sigmoid(r.sp[rr, :])
        r.dst[rr, :] = dpre.astype(BF)
        r.sacc[0] = r.sacc[0] + fold8(dpre)
        r.sacc[1] = r.sacc[1] + fold8(q * steps * decay_row)


    @pl.when(has_next)
    def _():
        back_copy(0).wait_recv()
        back_copy(1).wait_recv()

    def unmasked(grads, at, back):
        return jnp.where(at >= back, grads, 0.0) if back and not p.aligned else grads

    def conv_back(dpre, cw, width, out, fine=None):
        def body(t):
            grads = dpre[pl.ds(t, RT + 8), :]
            at = None if p.aligned else place(t, RT + 8, width)
            total = jnp.zeros((RT, width), F32)
            for k in range(p.taps):
                back = p.taps - 1 - k
                total = total + cw[k : k + 1, :] * unmasked(grads, at, back)[back : back + RT]
            hi, lo = parts(total, 2)
            out[pl.ds(t, RT), :] = hi
            if fine is not None:
                fine[pl.ds(t, RT), :] = lo

        rows_loop(tok, RT, body)

    conv_back(r.dsp, r.scw, s2, r.st, r.dsl)
    conv_back(r.dn, r.cw, w, r.wtd)


    def keep_out(rr, total):
        r.w_out[rr, :] = total

    def keep_gate(rr, total):
        r.w_gate[rr, :] = total

    def keep_va(rr, total):
        r.w_value[rr, 0 : p.cut] = total

    def keep_vb(rr, total):
        r.w_value[rr, p.cut : w] = total

    def keep_ss(rr, total):
        r.sq[rr, :] = total[:, 0:s2].astype(BF)
        r.sc[rr, :] = total[:, s2 : s2 + LANES]

    ar_service(12, 15)
    rs_take(p_out, 1, keep_out)
    r.pacc[...] = jnp.zeros((8, d), F32)
    r.sc[...] = jnp.zeros((tok, LANES), F32)

    def in_tile(n):
        nn = pl.ds(n, 256)
        r.mixer[:, 0:256] = (
            mm_rt(r.dgate[...], r.gw[nn, :])
            + mm_rt(r.wtd[...], r.vw[nn, :])
            + mm_rt(r.st[...], r.sw[nn, :])
            + mm(r.dst[...], r.swp[:, nn])
        )

        def body(t, j):
            rr = pl.ds(pl.multiple_of(j * SUB + t, RT), RT)
            grad = r.mixer[rr, 0:256]
            gx = grad * r.x[rr, nn].astype(F32)
            r.pacc[:, nn] = r.pacc[:, nn] + fold8(gx * wide(r.invin[rr, :], 2))
            gx = gx * r.pg[0:1, nn]
            r.sc[rr, :] = r.sc[rr, :] + (gx[:, 0:LANES] + gx[:, LANES:])
            low_grad = grad.astype(BF)
            for half in range(2):
                r.D[(n // LANES + half) * nsub + j, pl.ds(t, RT), :] = low_grad[:, half * LANES : (half + 1) * LANES]

        for j in range(nsub):
            rows_loop(SUB, RT, functools.partial(body, j=j))

    rows_loop(d // 2, 256, in_tile)
    ar_service(15, 16)
    rows_loop(d // 2, 256, lambda n: in_tile(pl.multiple_of(n + d // 2, 256)))

    def body(t):
        rr = pl.ds(t, L)
        r.sc[rr, :] = jnp.broadcast_to(jnp.sum(r.sc[rr, :], axis=1, keepdims=True), (L, LANES))

    rows_loop(tok, L, body)
    zx_send(1, r.sc)
    ar_service(16, 19)

    zs, sm = r.zs, r.sm.at[0]
    quarter = d // 4
    sm[...] = jnp.zeros((16, w), F32)

    def conv_sums(raw, dpre, width):
        cacc = r.cacc
        cacc[:, :, 0:width] = jnp.zeros((p.taps + 1, 8, width), F32)

        def body(t):
            win = raw[pl.ds(t, RT + HALO), :].astype(F32)
            grads = dpre[pl.ds(t, RT), :]
            at = None if p.aligned else place(t, RT, width)
            cacc[p.taps, :, 0:width] = cacc[p.taps, :, 0:width] + fold8(grads)
            for k in range(p.taps):
                back = p.taps - 1 - k
                term = unmasked(grads, at, back) * win[HALO - back : HALO - back + RT]
                cacc[k, :, 0:width] = cacc[k, :, 0:width] + fold8(term)

        rows_loop(tok, RT, body)
        return [jnp.sum(cacc[k, :, 0:width], axis=0, keepdims=True) for k in range(p.taps + 1)]

    sums = conv_sums(r.sraw, r.dsp, s2)
    for k in range(p.taps):
        zs[rank, 4 + k : 5 + k, 0:s2] = sums[k]
    for k in range(2):
        zs[rank, 4 + k : 5 + k, s2 : s2 + LANES] = sums[p.taps][:, k * LANES : (k + 1) * LANES]
    zs[rank, 6:8, s2 : s2 + LANES] = jnp.zeros((2, LANES), F32)
    gains = jnp.sum(r.pacc[...], axis=0, keepdims=True)
    for k in range(4):
        zs[rank, k : k + 1, :] = gains[:, k * quarter : (k + 1) * quarter]
    for off in range(1, tp):
        slot_copy(r.zs, r.zssem, TP, rank, tp, off).start()

    ar_service(19, 20)
    zx_take(1, r.sc)

    def body(t):
        rr = pl.ds(t, L)
        inv = r.invin[rr, :]
        r.coefo[rr, :] = inv * inv * inv * (r.sc[rr, 0:1] * (1.0 / d))

    rows_loop(tok, L, body)
    ar_service(20, 21)
    give = [
        pltpu.make_async_copy(src, dst, r.osem.at[i])
        for i, (src, dst) in enumerate(((r.w_out, r.o_out), (r.w_gate, r.o_gate), (r.w_value, r.o_value)))
    ]
    for s in range(2, p.nbits):
        rs_take(p_out, s, keep_out)
    give[0].start()
    ar_service(21, 23)
    rs_take(p_gate, 1, keep_gate)
    rs_finish(p_out)
    weight_grad(r.tb, r.wtd, r.g_out, w, nt)
    rs_send(p_va, 0)
    rs_send(p_vb, 0)
    ar_service(23, 25)
    full = (mm(r.tb[...], r.st[...]) + mm(r.tb[...], r.dsl[...])).astype(BF)
    for k in range(dp):
        r.g_ss[k, :, 0:s2] = full[k * p.crow : (k + 1) * p.crow, :]
    full = mm(r.tb[...], r.dst[...]).astype(BF)
    for k in range(dp):
        r.g_ss[k, :, s2 : s2 + LANES] = full[k * p.crow : (k + 1) * p.crow, :]
    rs_send(p_ss, 0)

    for off in range(1, tp):
        slot_copy(r.zs, r.zssem, TP, rank, tp, off).wait_recv()
    total = zs[0]
    for k in range(1, tp):
        total = total + zs[k]
    sm[8:16, 0:quarter] = total
    sums = conv_sums(r.vraw, r.dn, w)
    for k in range(p.taps + 1):
        sm[k : k + 1, :] = sums[k]
    sm[5:6, :] = jnp.sum(r.acc[0], axis=0, keepdims=True)
    sm[6:7, 0:LANES] = jnp.sum(r.sacc[0], axis=0, keepdims=True)
    sm[6:7, LANES : 2 * LANES] = jnp.sum(r.sacc[1], axis=0, keepdims=True)
    sm[7:8, 0:LANES] = mm_rt_fine(
        jnp.broadcast_to(jnp.sum(r.acc[1], axis=0, keepdims=True), (8, w)), r.E[...], 3
    )[0:1]
    sm_copy(0).start()

    ar_service(25, 27)
    late = ((p_va, keep_va), (p_vb, keep_vb), (p_ss, keep_ss))
    sm_take(0)
    for piece, out in late:
        rs_take(piece, 0, out)
    ar_service(27, 31)
    for s in range(2, p.nbits):
        rs_take(p_gate, s, keep_gate)
    give[1].start()
    ar_service(31, 38)
    at = 38
    for s in range(1, p.nbits):
        sm_take(s)
        for piece, out in late:
            rs_take(piece, s, out)
        if s < p.nbits - 1:
            ar_service(at, at + 7)
            at += 7
    give[2].start()

    def sq_copy(src, dst, ssem, rsem, to):
        return remote(src, dst, r.sqsem.at[ssem], r.sqsem.at[rsem], TP, to)

    sq_in = lambda src: sq_copy(src, r.sq_in, 0, 1, inward)
    sq_swap = lambda: sq_copy(r.sq_in, r.sq_x, 0, 2, inward)
    sq_out = lambda: sq_copy(r.sq_x, r.sq_x, 3, 4, outward)

    def sq_rows(fn):
        rows_loop(p.crow, RT, lambda t: fn(pl.ds(t, RT)))

    @pl.when(end)
    def _():
        sq_in(r.sq).start()

    ar_service(at, at + 2)

    @pl.when(jnp.logical_not(end))
    def _():
        sq_in(r.sq).wait_recv()

        def body(rr):
            r.sq_in[rr, :] = (r.sq_in[rr, :].astype(F32) + r.sq[rr, :].astype(F32)).astype(BF)

        sq_rows(body)
        if half_t > 2:

            @pl.when(jnp.logical_not(mid))
            def _():
                sq_in(r.sq_in).start()

        @pl.when(mid)
        def _():
            sq_swap().start()

    ar_service(at + 2, at + 4)
    at += 4

    @pl.when(mid)
    def _():
        sq_swap().wait()

        def body(rr):
            r.sq_x[rr, :] = (r.sq_in[rr, :].astype(F32) + r.sq_x[rr, :].astype(F32)).astype(BF)

        sq_rows(body)
        sq_out().start()


    for c in range(-(-p.crow // LANES)):
        width = min(LANES, p.crow - c * LANES)
        r.o_step[:, c * LANES : c * LANES + width] = r.sc[c * LANES : (c + 1) * LANES, :].T[0 : p.h, 0:width]

    total = r.sm[p.nbits]
    r.o_cw[...] = total[0 : p.taps]
    r.o_cb[...] = total[p.taps : p.taps + 1]
    r.o_ng[...] = total[5:6]
    r.o_sb[...] = total[6:7, 0 : p.h]
    r.o_dl[...] = total[6:7, LANES : LANES + p.h]
    r.o_sk[...] = total[7:8, 0 : p.h]
    r.o_scw[...] = total[12 : 12 + p.taps, 0:s2]
    for k in range(2):
        r.o_scb[:, k * LANES : (k + 1) * LANES] = total[12 + k : 13 + k, s2 : s2 + LANES]
    own = jnp.zeros((1, p.crow), F32)
    per = quarter // p.crow
    for k in range(dp):
        piece = total[8 + k // per : 9 + k // per, k % per * p.crow : (k % per + 1) * p.crow]
        own = own + jnp.where(me == k, piece, 0.0)
    r.o_pg[...] = own

    for c in few_gives[1:]:
        c.start()
    ar_service(at, last_step)

    @pl.when(jnp.logical_not(mid))
    def _():
        sq_in(r.sq).wait_send()
        sq_out().wait_recv()
        if half_t > 2:

            @pl.when(jnp.logical_not(end))
            def _():
                sq_out().start()

    @pl.when(jnp.logical_not(end))
    def _():
        sq_out().wait_send()

    def body(rr):
        r.o_state[rr, :] = r.sq_x[rr, :].astype(F32)

    sq_rows(body)
    few_gives[0].start()

    for s in range(last_step - FIN, 2 * nch):
        ar_finish(*divmod(s, nch))
    for s in range(last_step - KEPT, 2 * nch):
        ar_kept(*divmod(s, nch))
    for c in give + few_gives:
        c.wait()
    for piece in (p_gate, p_va, p_vb, p_ss):
        rs_finish(piece)
    for off in range(1, tp):
        zx_copy(0, off).wait_send()
        zx_copy(1, off).wait_send()
        slot_copy(r.zs, r.zssem, TP, rank, tp, off).wait_send()
    for s in range(p.nbits):
        sm_copy(s).wait_send()

    @pl.when(has_next)
    def _():
        halo_copy().wait_send()

    @pl.when(has_prev)
    def _():
        back_copy(0).wait_send()
        back_copy(1).wait_send()

    for k in range(1, p.reach + 1):

        @pl.when(ok_fwd(k, me))
        def _(k=k):
            bwd_copy(k).wait_send()


def on_device(
    mesh, x, lens, pg, gw, vw, sw, stepw, cw, cb, scw, scb, sb, dl, sk, ng, ow, og
):
    row = lambda a: a.reshape(1, -1)
    big = (x, gw, vw, sw, ow, og)
    small = dict(
        pg_in=pg, stepw=stepw.T, cw=cw, cb_in=cb, scw=scw, scb=row(scb), sb=row(sb), dl=row(dl),
        sk=row(sk), ng_in=ng,
    )
    p = Plan(mesh, x, lens, gw, sw, stepw.T, cw)
    scratch = scratch_of(p)
    for k, v in small.items():
        scratch[k] = pltpu.VMEM(v.shape, v.dtype)
    f = lambda *s: jax.ShapeDtypeStruct(s, F32)
    rows = jax.ShapeDtypeStruct((p.tok, p.d), BF)
    shapes = dict(
        o_block=rows, o_input=rows, o_pg=f(1, p.crow), o_gate=f(p.crow, p.w), o_value=f(p.crow, p.w),
        o_state=f(p.crow, p.s2), o_step=f(p.h, p.crow), o_cw=f(p.taps, p.w), o_cb=f(1, p.w),
        o_scw=f(p.taps, p.s2), o_scb=f(1, p.s2), o_sb=f(1, p.h), o_dl=f(1, p.h), o_sk=f(1, p.h),
        o_ng=f(1, p.w), o_out=f(p.crow, p.w),
    )
    few_out = tuple(reversed([k for k in shapes if k not in BY_COPY and k != STATE_OUT])) + (STATE_OUT,)
    few_out = few_out[::-1]
    for k in few_out:
        scratch[k] = pltpu.VMEM(shapes[k].shape, F32)
    scratch[FEW_SEM] = pltpu.SemaphoreType.DMA((2, max(len(small), len(few_out))))
    any_ = pl.BlockSpec(memory_space=pl.ANY)
    smem = pl.BlockSpec(memory_space=pltpu.SMEM)
    unnamed = tuple("s" + str(i) for i in range(len(big)))
    hbm = lambda keys: tuple(HBM + k if k in scratch else k for k in keys)
    names = unnamed + ("lens",) + hbm(small) + hbm(shapes) + tuple(scratch)
    outs = pl.pallas_call(
        functools.partial(kernel, p, names, tuple(small), few_out),
        out_shape=tuple(shapes.values()),
        in_specs=[any_] * len(big) + [smem] + [any_] * len(small),
        out_specs=[any_] * len(shapes),
        scratch_shapes=list(scratch.values()),
        compiler_params=pltpu.CompilerParams(
            collective_id=0, has_side_effects=True, vmem_limit_bytes=VMEM_BYTES
        ),
    )(*big, lens, *small.values())
    outs = deliver(outs)
    names = list(shapes)
    turned = (names.index(STEP_OUT), names.index(OUT_OUT))
    return tuple(o.T if i in turned else o for i, o in enumerate(outs))


STEP_OUT, OUT_OUT, STATE_OUT = "o_step", "o_out", "o_state"
HBM, FEW_SEM = "hbm_", "few_sem"
BY_COPY = ("o_block", "o_input", "o_gate", "o_value", "o_out")


def deliver(outs):
    count = len(outs)
    flat = [o.shape[0] == 1 for o in outs]
    shapes = [jax.ShapeDtypeStruct(o.shape[1:] if f else o.shape, o.dtype) for o, f in zip(outs, flat)]

    def body(*refs):
        ins, res, sems = refs[:count], refs[count : 2 * count], refs[2 * count]
        here = refs[2 * count + 1 : 3 * count + 1]
        rows = dict(zip([i for i in range(count) if flat[i]], refs[3 * count + 1 :]))
        reads = [pltpu.make_async_copy(ins[i], here[i], sems.at[0, i]) for i in range(count)]
        writes = [pltpu.make_async_copy(rows.get(i, here[i]), res[i], sems.at[1, i]) for i in range(count)]
        for c in reads:
            c.start()
        for i in range(count):
            reads[i].wait()
            if flat[i]:
                rows[i][...] = here[i][...].reshape(rows[i].shape)
            writes[i].start()
        for c in writes:
            c.wait()

    any_ = pl.BlockSpec(memory_space=pl.ANY)
    return pl.pallas_call(
        body,
        out_shape=shapes,
        in_specs=[any_] * count,
        out_specs=[any_] * count,
        scratch_shapes=[pltpu.SemaphoreType.DMA((2, count))]
        + [pltpu.VMEM(o.shape, o.dtype) for o in outs]
        + [pltpu.VMEM(s.shape, s.dtype) for s, f in zip(shapes, flat) if f],
        compiler_params=pltpu.CompilerParams(vmem_limit_bytes=VMEM_BYTES),
    )(*outs)


def solution(mesh):
    t = TP
    in_specs = (
        P(DP, None), P(), P(), P(None, t), P(None, t), P(), P(None, t), P(None, t), P(t), P(), P(),
        P(t), P(t), P(t), P(t), P(t, None), P(DP, None),
    )
    out_specs = (
        P(DP, None), P(DP, None), P(DP), P(DP, t), P(DP, t), P(DP, None), P(DP, t),
        P(None, t), P(t), P(), P(), P(t), P(t), P(t), P(t), P(t, DP),
    )
    return jax.shard_map(
        functools.partial(on_device, mesh), mesh=mesh, in_specs=in_specs, out_specs=out_specs, check_vma=False
    )
```

```python
import functools
import types

import jax
import jax.numpy as jnp
from jax import lax
from jax.experimental import pallas as pl
from jax.experimental.pallas import tpu as pltpu
from jax.sharding import PartitionSpec as P

F32 = jnp.float32
BF = jnp.bfloat16
MAXLEN = 2048
HEADDIM = 64
L = 128
RT = 32
LANES = 128
SUB = 256
HALO = 16
EPS = 1e-05
NEG = -1e30
VMEM_BYTES = 64 * 1024 * 1024 - 4096
DP = "dp"
TP = "tensor"


def mm(a, b):
    return lax.dot_general(a, b, (((1,), (0,)), ((), ())), preferred_element_type=F32)


def mm_rt(a, b):
    return lax.dot_general(a, b, (((1,), (1,)), ((), ())), preferred_element_type=F32)


def mm_lt(a, b):
    return lax.dot_general(a, b, (((0,), (0,)), ((), ())), preferred_element_type=F32)


def parts(a, n):
    out = []
    for _ in range(n - 1):
        hi = a.astype(BF)
        out.append(hi)
        a = a - hi.astype(F32)
    out.append(a.astype(BF))
    return out


def mm_fine(a, b, n=2):
    total = None
    for p in parts(a, n):
        t = mm(p, b)
        total = t if total is None else total + t
    return total


def mm_fine_right(a, b, n=3):
    total = None
    for p in parts(b, n):
        t = mm(a, p)
        total = t if total is None else total + t
    return total


def mm_rt_fine(a, b, n=3):
    total = None
    for p in parts(a, n):
        t = mm_rt(p, b)
        total = t if total is None else total + t
    return total


def wide(a, n):
    return jnp.concatenate([a] * n, axis=1) if n > 1 else a


def fold8(a):
    total = a[0:8]
    for i in range(8, a.shape[0], 8):
        total = total + a[i : i + 8]
    return total


def rows_loop(n, size, fn):
    def step(i, carry):
        fn(pl.multiple_of(i * size, size))
        return carry

    lax.fori_loop(0, n // size, step, 0)


def sigmoid(v):
    return 0.5 * jnp.tanh(0.5 * v) + 0.5


def silu_parts(v):
    sig = sigmoid(v)
    return v * sig, sig * (1.0 + v * (1.0 - sig))


class Plan:
    def __init__(self, mesh, x, lens, gw, sw, stepw, cw):
        self.dp = mesh.shape[DP]
        self.tp = mesh.shape[TP]
        self.tok, self.d = x.shape
        self.w = gw.shape[1]
        self.h = stepw.shape[0]
        self.s2 = sw.shape[1]
        self.ns = self.s2 // 2
        self.taps = cw.shape[0]
        self.nseq = lens.shape[0]
        self.total = self.tok * self.dp
        self.nb = self.tok // L
        self.pairs = self.h // 2
        self.nt = 256 if self.w % 256 == 0 else 128
        self.aligned = self.nseq * MAXLEN == self.total and MAXLEN % self.tok == 0
        self.group = MAXLEN // self.tok
        if self.aligned:
            self.reach = 1
        else:
            self.reach = min(-(-(MAXLEN - 1) // self.tok), self.dp - 1)
        self.srows = self.ns if self.aligned else self.ns + HALO
        self.nbits = self.dp.bit_length() - 1
        self.nc = self.d // LANES
        self.nsub = self.tok // SUB
        self.nch = self.nc * self.nsub
        self.cut = self.w // LANES // 2 * LANES
        self.crow = self.d // self.dp
        bits = list(range(self.nbits))
        self.order_a = bits
        self.order_b = bits[:1] + bits[1:][::-1]


def scratch_of(p):
    tok, d, w, ns, s2, nb, dp, tp = p.tok, p.d, p.w, p.ns, p.s2, p.nb, p.dp, p.tp
    v = lambda *s, t=BF: pltpu.VMEM(s, t)
    dma = lambda *s: pltpu.SemaphoreType.DMA(s)
    return dict(
        x=v(tok, d), gw=v(d, w), vw=v(d, w), sw=v(d, s2), ow=v(w, d), og=v(tok, d),
        in_sem=dma(6), pg=v(1, d, t=F32), cb=v(1, w, t=F32), ng=v(1, w, t=F32),
        swp=v(LANES, d), small=v(8, LANES, t=F32), E=v(LANES, w), ske=v(8, w, t=F32),
        hx=v(HALO, d), nx=v(tok + HALO, d), tb=v(d, tok), invin=v(tok, LANES, t=F32),
        vraw=v(tok + HALO, w), sraw=v(tok + HALO, s2), vgr=v(tok, w), sgr=v(tok, s2),
        val=v(tok, w), st=v(tok, s2), stT=v(s2, tok), gate=v(tok, w),
        sp=v(tok, LANES, t=F32), steps=v(tok, LANES, t=F32),
        cum=v(tok, LANES, t=F32), cumT=v(LANES, tok, t=F32),
        stepe=v(tok, w, t=F32), care=v(tok, w), taile=v(tok, w),
        facr=v(8 * nb, w, t=F32),
        wtd=v(tok, w), tw=v(tok, w), ends=v(nb, ns, w, t=F32), run=v(ns, w, t=F32),
        D=v(max(nb * p.pairs, p.nch), SUB, LANES), mixer=v(tok, w, t=F32), cp=v(tok, w), gn=v(tok, w),
        dn=v(tok + 8, w, t=F32), STb=v(nb, ns, w),
        sc=v(tok, LANES, t=F32),
        invo=v(tok, LANES, t=F32), coefo=v(tok, LANES, t=F32),
        dgate=v(tok, w), sdm=v(tok, w), rc=v(tok, LANES, t=F32),
        colT=v(LANES, L, t=F32), gsc=v(L, L, t=F32), rs=v(L, LANES, t=F32),
        gBC=v(tok, s2, t=F32), gf=v(8 * nb, w, t=F32), gtl=v(ns, w), dsp=v(tok + 8, s2, t=F32),
        dsl=v(tok, s2), dst=v(tok, LANES),
        acc=v(2, 8, w, t=F32), cacc=v(p.taps + 1, 8, max(w, s2), t=F32), pacc=v(8, d, t=F32),
        sacc=v(4, 8, LANES, t=F32),
        halo_sem=dma(6),
        fbuf=v(p.srows, w), fin=v(max(p.reach, 1), p.srows, w), fsem=dma(2, max(p.reach, 1)),
        bin=v(max(p.reach, 1), p.srows, w), bsem=dma(2, max(p.reach, 1)),
        zx=v(2, tp, 2 * nb, LANES, t=F32), zsem=dma(2, 2, tp),
        zs=v(tp, 8, d // 4, t=F32), zssem=dma(2, tp),
        sm=v(p.nbits + 1, 16, w, t=F32), sm_in=v(p.nbits, 16, w, t=F32), smsem=dma(2, p.nbits),
        Pf=v(p.nch, SUB, LANES), ar_a=v(2, p.nch, SUB, LANES), ar_b=v(p.nch, SUB, LANES),
        arsem=dma(2, 6, p.nch),
        w_gate=v(p.crow, w, t=F32), w_value=v(p.crow, w, t=F32), w_out=v(p.crow, w, t=F32), osem=dma(3),
        sq=v(p.crow, s2), sq_in=v(p.crow, s2), sq_x=v(p.crow, s2), sqsem=dma(5),
        g_out=v(dp, p.crow, w), r_out=v(dp - 1, p.crow, w), s_out=dma(2, dp),
        g_ss=v(dp, p.crow, s2 + LANES), g_gate=v(dp, p.crow, w), r_gate=v(dp - 1, p.crow, w), s_gate=dma(2, dp),
        r_va=v(dp - 1, p.crow, p.cut), s_va=dma(2, dp),
        r_vb=v(dp - 1, p.crow, w - p.cut), s_vb=dma(2, dp),
        r_ss=v(dp - 1, p.crow, s2 + LANES), s_ss=dma(2, dp),
    )


def kernel(p, names, few_in, few_out, *refs):
    r = types.SimpleNamespace(**dict(zip(names, refs)))
    by_name = dict(zip(names, refs))
    few_loads = [
        pltpu.make_async_copy(by_name[HBM + k], by_name[k], r.few_sem.at[0, i]) for i, k in enumerate(few_in)
    ]
    few_gives = [
        pltpu.make_async_copy(by_name[k], by_name[HBM + k], r.few_sem.at[1, i]) for i, k in enumerate(few_out)
    ]
    big = (r.x, r.gw, r.vw, r.sw, r.ow, r.og)
    sources = refs[: len(big)]
    tok, d, w, ns, s2, nb, dp, tp, pairs = p.tok, p.d, p.w, p.ns, p.s2, p.nb, p.dp, p.tp, p.pairs
    me = lax.axis_index(DP)
    rank = lax.axis_index(TP)
    first = me * tok
    wl = w // LANES
    inner = w * tp
    nt = p.nt

    def bit(v, b):
        return lax.rem(v // (2**b), 2)

    def remote(src, dst, ssem, rsem, axis, at):
        return pltpu.make_async_remote_copy(
            src_ref=src,
            dst_ref=dst,
            send_sem=ssem,
            recv_sem=rsem,
            device_id={axis: at},
            device_id_type=pl.DeviceIdType.MESH,
        )

    def load(at):
        return pltpu.make_async_copy(sources[at], big[at], r.in_sem.at[at])

    X, GW, VW, SW, OW, OG = range(len(big))
    load(X).start()
    for c in few_loads:
        c.start()
    for at in (VW, SW):
        load(at).start()

    barrier = pltpu.get_barrier_semaphore()
    for off in range(1, tp):
        pl.semaphore_signal(
            barrier, inc=1, device_id={TP: lax.rem(rank + off, tp)}, device_id_type=pl.DeviceIdType.MESH
        )
    for off in range(1, dp):
        pl.semaphore_signal(
            barrier, inc=1, device_id={DP: lax.rem(me + off, dp)}, device_id_type=pl.DeviceIdType.MESH
        )

    ahead = lax.rem(me, p.group)
    behind = p.group - 1 - ahead
    has_prev = ahead > 0 if p.aligned else me > 0
    has_next = behind > 0 if p.aligned else me < dp - 1
    starts = [jnp.int32(0)]
    for k in range(p.nseq - 1):
        starts.append(starts[-1] + r.lens[k])

    def start_of(g):
        at = jnp.zeros_like(g) if getattr(g, "shape", ()) else jnp.int32(0)
        for s in starts[1:]:
            at = jnp.where(g >= s, s, at)
        return at

    def place(t0, rows, width):
        g = first + t0 + lax.broadcasted_iota(jnp.int32, (rows, width), 0)
        return g - start_of(g)

    for c in few_loads:
        c.wait()
    row_w = lax.broadcasted_iota(jnp.int32, (LANES, w), 0)
    lane_w = lax.broadcasted_iota(jnp.int32, (LANES, w), 1)
    r.E[...] = jnp.where(lane_w // HEADDIM == row_w, 1.0, 0.0).astype(BF)
    r.small[...] = jnp.zeros((8, LANES), F32)
    r.small[0:1, 0 : p.h] = r.sb[...]
    r.small[1:2, 0 : p.h] = r.dl[...]
    r.small[2:3, 0 : p.h] = r.sk[...]
    r.ske[...] = mm_fine(jnp.broadcast_to(r.small[2:3, :], (8, LANES)), r.E[...], 3)
    r.swp[...] = jnp.zeros((LANES, d), BF)
    r.swp[0 : p.h, :] = r.stepw[...]
    r.pg[...] = r.pg_in[...].reshape(1, d)
    r.cb[...] = r.cb_in[...].reshape(1, w)
    r.ng[...] = r.ng_in[...].reshape(1, w)
    skip_row = r.ske[0:1, :]
    bias_row = r.small[0:1, :]
    decay_row = -jnp.exp(r.small[1:2, :])
    lane_l = lax.broadcasted_iota(jnp.int32, (L, LANES), 1)
    row_l = lax.broadcasted_iota(jnp.int32, (L, LANES), 0)

    load(X).wait()
    for at in (GW, OG, OW):
        load(at).start()
    pl.semaphore_wait(barrier, tp - 1 + dp - 1)

    def halo_copy():
        return remote(
            r.x.at[pl.ds(tok - HALO, HALO), :], r.hx, r.halo_sem.at[0], r.halo_sem.at[1],
            DP, jnp.minimum(me + 1, dp - 1),
        )

    @pl.when(has_next)
    def _():
        halo_copy().start()

    @pl.when(jnp.logical_not(has_prev))
    def _():
        r.hx[...] = jnp.zeros((HALO, d), BF)

    def ok_fwd(k, at):
        c = at >= k
        return jnp.logical_and(c, lax.rem(at, p.group) >= k) if p.aligned else c

    def ok_bwd(k, at):
        c = at + k < dp
        return jnp.logical_and(c, lax.rem(at, p.group) + k < p.group) if p.aligned else c

    def fwd_copy(k):
        return remote(
            r.fbuf, r.fin.at[k - 1], r.fsem.at[0, k - 1], r.fsem.at[1, k - 1], DP,
            jnp.minimum(me + k, dp - 1),
        )

    def bwd_copy(k):
        return remote(
            r.fbuf, r.bin.at[k - 1], r.bsem.at[0, k - 1], r.bsem.at[1, k - 1], DP,
            jnp.maximum(me - k, 0),
        )

    for k in range(1, p.reach + 1):

        @pl.when(jnp.logical_not(ok_fwd(k, me)))
        def _(k=k):
            r.fin[k - 1] = jnp.zeros((p.srows, w), BF)

        @pl.when(jnp.logical_not(ok_bwd(k, me)))
        def _(k=k):
            r.bin[k - 1] = jnp.zeros((p.srows, w), BF)

    def own_factor():
        f = r.facr[0:1, :]
        for c in range(1, nb):
            f = f * r.facr[8 * c : 8 * c + 1, :]
        return f


    def pass_on(copy, slots, first):
        f = own_factor()

        def body(t):
            rr = pl.ds(t, RT)
            state = r.run[rr, :]
            if not first:
                state = state + f * slots[0, rr, :].astype(F32)
            r.fbuf[rr, :] = state.astype(BF)

        rows_loop(ns, RT, body)
        copy(1).start()

    def send_states(copy, turn, has):
        if p.aligned:

            @pl.when(jnp.logical_and(turn == 0, turn < p.group - 1))
            def _():
                pass_on(copy, None, True)

            return

        def body(t):
            rr = pl.ds(t, RT)
            r.fbuf[rr, :] = r.run[rr, :].astype(BF)

        rows_loop(ns, RT, body)
        r.fbuf[ns : ns + HALO, :] = jnp.broadcast_to(own_factor(), (HALO, w)).astype(BF)
        for k in range(1, p.reach + 1):

            @pl.when(has(k))
            def _(k=k):
                copy(k).start()

    def relay_states(copy, slots, turn, lo, hi):
        if p.aligned:
            hi = min(hi, p.group - 1)
            if lo < hi:

                @pl.when(jnp.logical_and(turn >= lo, turn < hi))
                def _():
                    copy(1).wait_recv()
                    pass_on(copy, slots, False)

    def receive_states(copy, slots, turn, has):
        if p.aligned:

            @pl.when(jnp.logical_and(turn == p.group - 1, turn > 0))
            def _():
                copy(1).wait_recv()

            def body(t):
                rr = pl.ds(t, RT)
                r.run[rr, :] = slots[0, rr, :].astype(F32)

            rows_loop(ns, RT, body)
            return

        for k in range(1, p.reach + 1):

            @pl.when(has(k))
            def _(k=k):
                copy(k).wait_recv()

        def body(t):
            rr = pl.ds(t, RT)
            total = jnp.zeros((RT, w), F32)
            f = jnp.ones((1, w), F32)
            for k in range(p.reach):
                total = total + f * slots[k, rr, :].astype(F32)
                f = f * slots[k, ns : ns + HALO, :].astype(F32)[0:1]
            r.run[rr, :] = total

        rows_loop(ns, RT, body)

    def ar_sems(ph, kind, i):
        return r.arsem.at[ph, kind, i]

    def cols(i):
        return pl.ds(pl.multiple_of(i * LANES, LANES), LANES)

    nsub = p.nsub
    ar_src = (r.Pf, r.D)

    nch = p.nch

    def columns(i):
        return cols(i // nsub)

    def row0(i):
        return pl.multiple_of(lax.rem(i, nsub) * SUB, SUB) if isinstance(i, jax.Array) else i % nsub * SUB

    ar_dst = (r.o_block, r.o_input)

    half_t = tp // 2
    mid = jnp.logical_or(rank == half_t - 1, rank == half_t)
    inward = jnp.where(rank < half_t, rank + 1, rank - 1)
    outward = jnp.clip(jnp.where(rank < half_t, rank - 1, rank + 1), 0, tp - 1)
    end = jnp.logical_or(rank == 0, rank == tp - 1)
    ar_across = (r.ar_b, r.Pf)

    def ar_a(ph, i):
        return r.ar_a.at[ph, i]

    def ar_in(ph, i, src):
        return remote(src, ar_a(ph, i), ar_sems(ph, 0, i), ar_sems(ph, 1, i), TP, inward)

    def ar_swap(ph, i):
        return remote(
            ar_a(ph, i), ar_across[ph].at[i], ar_sems(ph, 0, i), ar_sems(ph, 2, i), TP, inward
        )

    def ar_out(ph, i, src):
        return remote(src, ar_a(ph, i), ar_sems(ph, 3, i), ar_sems(ph, 4, i), TP, outward)

    def ar_keep(ph, i, src):
        return pltpu.make_async_copy(src, ar_dst[ph].at[pl.ds(row0(i), SUB), columns(i)], ar_sems(ph, 5, i))

    def each_rows(i, fn):
        base = row0(i)
        rows_loop(SUB, L, lambda t: fn(pl.ds(t, L), pl.ds(pl.multiple_of(base + t, L), L)))

    def ar_start(ph, i):
        @pl.when(end)
        def _():
            ar_in(ph, i, ar_src[ph].at[i]).start()

    def ar_add(ph, i):
        @pl.when(end)
        def _():
            ar_in(ph, i, ar_a(ph, i)).wait_send()
            to, at = divmod(ph * nch + i + DEPTH, nch)
            if to < 2:
                ar_in(to, at, ar_src[to].at[at]).start()

        @pl.when(jnp.logical_not(end))
        def _():
            ar_in(ph, i, ar_a(ph, i)).wait_recv()

            def body(q, rr):
                r.ar_a[ph, i, q, :] = (r.ar_a[ph, i, q, :].astype(F32) + ar_src[ph][i, q, :].astype(F32)).astype(BF)

            each_rows(i, body)
            if half_t > 2:

                @pl.when(jnp.logical_not(mid))
                def _():
                    ar_in(ph, i, ar_a(ph, i)).start()

            @pl.when(mid)
            def _():
                ar_swap(ph, i).start()

    def ar_done(ph, i):
        @pl.when(mid)
        def _():
            ar_swap(ph, i).wait()
            got = ar_across[ph]

            def body(q, rr):
                total = r.ar_a[ph, i, q, :].astype(F32) + got[i, q, :].astype(F32)
                xt = r.x[rr, columns(i)].astype(F32)
                if ph == 0:
                    res = xt + total * r.invo[rr, :]
                else:
                    f = total * r.pg[0:1, columns(i)]
                    res = r.og[rr, columns(i)].astype(F32) + r.invin[rr, :] * f - xt * r.coefo[rr, :]
                got[i, q, :] = res.astype(BF)

            each_rows(i, body)
            ar_out(ph, i, got.at[i]).start()
            ar_keep(ph, i, got.at[i]).start()

        if half_t > 2:

            @pl.when(jnp.logical_not(jnp.logical_or(mid, end)))
            def _():
                here = ar_a(ph, i)
                ar_in(ph, i, here).wait_send()
                ar_out(ph, i, here).wait_recv()
                ar_out(ph, i, here).start()
                ar_keep(ph, i, here).start()

    def ar_finish(ph, i):
        here = ar_a(ph, i)

        @pl.when(end)
        def _():
            ar_out(ph, i, here).wait_recv()
            ar_keep(ph, i, here).start()

        @pl.when(jnp.logical_not(end))
        def _():
            ar_out(ph, i, here).wait_send()

    def ar_kept(ph, i):
        ar_keep(ph, i, ar_a(ph, i)).wait()

    LAG = 3
    DEPTH = 4
    FIN = LAG + 6
    KEPT = FIN + 4
    last_step = 2 * nch + LAG

    def ar_service(s0, s1):
        for s in range(s0, min(s1, last_step)):
            if s < 2 * nch:
                ar_add(*divmod(s, nch))
            if s >= LAG:
                ar_done(*divmod(s - LAG, nch))
            if s >= FIN:
                ar_finish(*divmod(s - FIN, nch))
            if s >= KEPT:
                ar_kept(*divmod(s - KEPT, nch))

    p_out = (r.g_out, 0, w, r.r_out, r.s_out, p.order_a)
    p_gate = (r.g_gate, 0, w, r.r_gate, r.s_gate, p.order_b)
    p_va = (r.g_out, 0, p.cut, r.r_va, r.s_va, p.order_a)
    p_vb = (r.g_out, p.cut, w, r.r_vb, r.s_vb, p.order_b)
    p_ss = (r.g_ss, 0, s2 + LANES, r.r_ss, r.s_ss, p.order_a)

    def rs_copy(piece, s, idx):
        g, lo, hi, got, sems, order = piece
        base = sum(dp // 2 ** (q + 1) for q in range(s))
        k = jnp.int32(0)
        for q in order[:s]:
            k = k + bit(me, q) * 2**q
        rem = [b for b in range(p.nbits) if b not in order[: s + 1]]
        for n, b in enumerate(rem):
            k = k + ((idx >> n) & 1) * 2**b
        b = order[s]
        mine = bit(me, b)
        keep = k + mine * 2**b
        send = k + (1 - mine) * 2**b
        src = g.at[send] if hi - lo == g.shape[2] else g.at[send, :, pl.ds(lo, hi - lo)]
        copy = remote(
            src, got.at[base + idx], sems.at[0, base + idx], sems.at[1, base + idx],
            DP, me + (1 - 2 * mine) * 2**b,
        )
        return copy, keep, base + idx

    def rs_send(piece, s):
        for idx in range(dp // 2 ** (s + 1)):
            rs_copy(piece, s, idx)[0].start()

    def rs_take(piece, s, out=None):
        g, lo, hi, got = piece[:4]
        last = s == p.nbits - 1
        for idx in range(dp // 2 ** (s + 1)):
            copy, keep, at = rs_copy(piece, s, idx)
            copy.wait_recv()

            def body(t, keep=keep, at=at):
                rr = pl.ds(t, RT)
                total = g[keep, rr, lo:hi].astype(F32) + got[at, rr, :].astype(F32)
                if last:
                    out(rr, total)
                else:
                    g[keep, rr, lo:hi] = total.astype(BF)

            rows_loop(p.crow, RT, body)
        if not last:
            rs_send(piece, s + 1)

    def rs_finish(piece):
        for s in range(p.nbits):
            for idx in range(dp // 2 ** (s + 1)):
                rs_copy(piece, s, idx)[0].wait_send()

    def zx_copy(which, off):
        return remote(
            r.zx.at[which, rank], r.zx.at[which, rank], r.zsem.at[which, 0, off], r.zsem.at[which, 1, off],
            TP, lax.rem(rank + off, tp),
        )

    def zx_send(which, src):
        for c in range(nb):
            turned = src[c * L : (c + 1) * L, :].T
            r.zx[which, rank, c : c + 1, :] = turned[0:1]
            r.zx[which, rank, nb + c : nb + c + 1, :] = turned[1:2]
        for off in range(1, tp):
            zx_copy(which, off).start()

    def zx_take(which, dst):
        for off in range(1, tp):
            zx_copy(which, off).wait_recv()
        total = r.zx[which, 0]
        for k in range(1, tp):
            total = total + r.zx[which, k]
        for c in range(nb):
            first = jnp.broadcast_to(total[c : c + 1], (LANES, L))
            second = jnp.broadcast_to(total[nb + c : nb + c + 1], (LANES, L))
            dst[c * L : (c + 1) * L, :] = jnp.where(row_l == 0, first, second).T

    def sm_copy(s):
        mine = bit(me, s)
        return remote(
            r.sm.at[s], r.sm_in.at[s], r.smsem.at[0, s], r.smsem.at[1, s], DP, me + (1 - 2 * mine) * 2**s
        )

    def sm_take(s):
        sm_copy(s).wait_recv()
        r.sm[s + 1] = r.sm[s] + r.sm_in[s]
        if s + 1 < p.nbits:
            sm_copy(s + 1).start()

    def slot_copy(buf, sems, axis, at, count, off):
        return remote(
            buf.at[at], buf.at[at], sems.at[0, off], sems.at[1, off], axis, lax.rem(at + off, count)
        )

    def norm_rows(src, s0, dst0, rows):
        xf = src[pl.ds(s0, rows), :].astype(F32)
        inv = lax.rsqrt(jnp.mean(xf * xf, axis=1, keepdims=True) + EPS)
        r.nx[pl.ds(dst0, rows), :] = (xf * inv * r.pg[...]).astype(BF)
        return inv

    def body(t):
        inv = norm_rows(r.x, t, pl.multiple_of(t + HALO, HALO), RT)
        r.invin[pl.ds(t, RT), :] = jnp.broadcast_to(inv, (RT, LANES))

    rows_loop(tok, RT, body)

    @pl.when(has_prev)
    def _():
        halo_copy().wait_recv()

    norm_rows(r.hx, 0, 0, HALO)
    load(VW).wait()
    load(SW).wait()

    def body(n):
        nn = pl.ds(n, nt)
        r.vraw[:, nn] = mm(r.nx[...], r.vw[:, nn]).astype(BF)

    rows_loop(w, nt, body)
    r.sraw[...] = mm(r.nx[...], r.sw[...]).astype(BF)
    r.sp[...] = mm_rt(r.nx[HALO : HALO + tok, :], r.swp[...]).astype(BF).astype(F32) + bias_row

    def conv(raw, cw, cb, width, val, grad):
        def body(t):
            win = raw[pl.ds(t, RT + HALO), :].astype(F32)
            at = None if p.aligned else place(t, RT, width)
            total = jnp.broadcast_to(cb[...], (RT, width))
            for k in range(p.taps):
                back = p.taps - 1 - k
                tap = win[HALO - back : HALO - back + RT]
                if back and not p.aligned:
                    tap = jnp.where(at >= back, tap, 0.0)
                total = total + cw[k : k + 1, :] * tap
            act, slope = silu_parts(total)
            val[pl.ds(t, RT), :] = act.astype(BF)
            grad[pl.ds(t, RT), :] = slope.astype(BF)

        rows_loop(tok, RT, body)

    conv(r.sraw, r.scw, r.scb, s2, r.st, r.sgr)
    conv(r.vraw, r.cw, r.cb, w, r.val, r.vgr)

    for c in range(nb):
        r.stT[:, c * L : (c + 1) * L] = r.st[c * L : (c + 1) * L, :].T

    tri = jnp.where(row_l >= lane_l, 1.0, 0.0).astype(BF)
    for c in range(nb):
        rr = slice(c * L, (c + 1) * L)
        b0 = first + c * L
        pre = r.sp[rr, :]
        steps = jnp.maximum(pre, 0.0) + jnp.log1p(jnp.exp(-jnp.abs(pre)))
        cum = mm_fine_right(tri, decay_row * steps, 3)
        r.steps[rr, :] = steps
        r.cum[rr, :] = cum
        r.cumT[:, rr] = cum.T
        car = jnp.exp(cum)
        tail = jnp.exp(cum[L - 1 : L, :] - cum)
        if not p.aligned:
            g = b0 + row_l
            car = jnp.where(start_of(g) < b0, car, 0.0)
            tail = jnp.where(g >= start_of(b0 + L - 1), tail, 0.0)
        r.invo[rr, :] = car
        r.coefo[rr, :] = tail
        last = mm_fine(car[L - 8 : L, :], r.E[...], 2)[7:8]
        r.facr[8 * c : 8 * c + 8, :] = jnp.broadcast_to(last, (8, w))

    def body(n):
        nn = pl.ds(n, nt)
        r.stepe[:, nn] = mm_fine(r.steps[...], r.E[:, nn], 2)
        r.care[:, nn] = mm(r.invo[...].astype(BF), r.E[:, nn]).astype(BF)
        r.taile[:, nn] = mm(r.coefo[...].astype(BF), r.E[:, nn]).astype(BF)

    rows_loop(w, nt, body)

    def body(t):
        rr = pl.ds(t, RT)
        weighted = r.val[rr, :].astype(F32) * r.stepe[rr, :]
        r.wtd[rr, :] = weighted.astype(BF)
        r.tw[rr, :] = (weighted * r.taile[rr, :].astype(F32)).astype(BF)

    rows_loop(tok, RT, body)

    r.run[...] = jnp.zeros((ns, w), F32)
    for c in range(nb):
        rr = slice(c * L, (c + 1) * L)
        r.ends[c] = mm(r.stT[0:ns, rr], r.tw[rr, :])
        f = r.facr[8 * c : 8 * c + 1, :]

        def body(t, c=c, f=f):
            q = pl.ds(t, RT)
            r.run[q, :] = r.ends[c, q, :] + f * r.run[q, :]

        rows_loop(ns, RT, body)
    send_states(fwd_copy, ahead, lambda k: ok_bwd(k, me))

    def in_block(c):
        rr = pl.ds(pl.multiple_of(c * L, L), L)
        b_rows = r.st[rr, 0:ns]
        c_rows = r.st[rr, ns:s2]
        return rr, b_rows, c_rows, mm_rt(c_rows, b_rows)

    def within(c, carry):
        rr, b_rows, c_rows, scores = in_block(c)
        gt = first + c * L + row_l
        gs = first + c * L + lane_l
        keep = gs <= gt
        if not p.aligned:
            keep = jnp.logical_and(keep, gs >= start_of(gt))
        bias = jnp.where(keep, 0.0, NEG)
        cum = r.cum[rr, :]
        cumt = r.cumT[:, rr]
        for pr in range(pairs):
            decays, mixes = [], []
            for h in (2 * pr, 2 * pr + 1):
                dec = jnp.exp(cum[:, h : h + 1] - cumt[h : h + 1, :] + bias)
                dec = dec.astype(BF)
                decays.append(dec)
                mixes.append((dec.astype(F32) * scores).astype(BF))
            r.D[c * pairs + pr] = jnp.concatenate(decays, axis=0)
            both = mm(jnp.concatenate(mixes, axis=0), r.wtd[rr, pr * LANES : (pr + 1) * LANES])
            r.mixer[rr, pr * LANES : (pr + 1) * LANES] = jnp.where(lane_l < HEADDIM, both[0:L], both[L:])
        return carry

    lax.fori_loop(0, 1, within, 0)
    relay_states(fwd_copy, r.fin, ahead, 1, 2)
    lax.fori_loop(1, nb, within, 0)

    load(GW).wait()

    def body(n):
        nn = pl.ds(n, nt)
        r.gate[:, nn] = mm(r.nx[HALO : HALO + tok, :], r.gw[:, nn]).astype(BF)

    rows_loop(w, nt, body)

    load(OG).wait()
    load(OW).wait()

    def body(n):
        nn = pl.ds(n, nt)
        r.dn[0:tok, nn] = mm_rt(r.og[...], r.ow[nn, :])

    rows_loop(w, nt, body)

    relay_states(fwd_copy, r.fin, ahead, 2, p.group)
    receive_states(fwd_copy, r.fin, ahead, lambda k: ok_fwd(k, me))
    for c in range(nb):
        rr = slice(c * L, (c + 1) * L)
        f = r.facr[8 * c : 8 * c + 1, :]

        def body(t, c=c, f=f):
            q = pl.ds(t, RT)
            now = r.run[q, :]
            hi, lo = parts(now, 2)
            r.STb[c, q, :] = hi
            r.gtl[q, :] = lo
            r.run[q, :] = r.ends[c, q, :] + f * now
            r.ends[c, q, :] = now

        rows_loop(ns, RT, body)
        proj = mm(r.st[rr, ns:s2], r.STb[c]) + mm(r.st[rr, ns:s2], r.gtl[...])
        proj = proj * r.care[rr, :].astype(F32)
        r.cp[rr, :] = proj.astype(BF)
        r.mixer[rr, :] = r.mixer[rr, :] + proj

    lane_t = lax.broadcasted_iota(jnp.int32, (RT, LANES), 1)

    def body(t):
        rr = pl.ds(t, RT)
        mixer = r.mixer[rr, :] + skip_row * r.val[rr, :].astype(F32)
        gate = r.gate[rr, :].astype(F32)
        gated = mixer * (gate * sigmoid(gate))
        gained = gated * r.ng[...]
        r.mixer[rr, :] = mixer
        r.gn[rr, :] = gained.astype(BF)
        squares = jnp.sum(gated * gated, axis=1, keepdims=True)
        cross = jnp.sum(r.dn[rr, :] * gained, axis=1, keepdims=True)
        r.sc[rr, :] = jnp.where(lane_t == 0, squares, jnp.where(lane_t == 1, cross, 0.0))

    rows_loop(tok, RT, body)
    zx_send(0, r.sc)

    def out_tile(n):
        nn = pl.ds(n, 256)
        full = mm(r.gn[...], r.ow[:, nn]).astype(BF)
        for half in range(2):
            for j in range(nsub):
                at = (n // LANES + half) * nsub + j
                r.Pf[at] = full[j * SUB : (j + 1) * SUB, half * LANES : (half + 1) * LANES]

    per_tile = 2 * nsub
    lead = -(-DEPTH // per_tile)
    for n in range(lead):
        out_tile(n * 256)
        for i in range(n * per_tile, min((n + 1) * per_tile, DEPTH)):
            ar_start(0, i)
    rows_loop(d - lead * 256, 256, lambda n: out_tile(pl.multiple_of(n + lead * 256, 256)))

    for c in range(nb):
        r.tb[:, c * L : (c + 1) * L] = r.og[c * L : (c + 1) * L, :].T

    zx_take(0, r.sc)

    def body(t):
        rr = pl.ds(t, L)
        inv = lax.rsqrt(r.sc[rr, 0:1] * (1.0 / inner) + EPS)
        r.invo[rr, :] = jnp.broadcast_to(inv, (L, LANES))
        r.coefo[rr, :] = jnp.broadcast_to(inv * inv * inv * r.sc[rr, 1:2] * (1.0 / inner), (L, LANES))

    rows_loop(tok, L, body)

    r.acc[...] = jnp.zeros((2, 8, w), F32)

    def body(t):
        rr = pl.ds(t, RT)
        mixer = r.mixer[rr, :]
        act, slope = silu_parts(r.gate[rr, :].astype(F32))
        gated = mixer * act
        inv = wide(r.invo[rr, :], wl)
        coef = wide(r.coefo[rr, :], wl)
        dn = r.dn[rr, :]
        scaled = gated * inv
        dgated = inv * (dn * r.ng[...]) - gated * coef
        dmix = dgated * act
        val = r.val[rr, :].astype(F32)
        r.dgate[rr, :] = (dgated * mixer * slope).astype(BF)
        r.gn[rr, :] = (scaled * r.ng[...]).astype(BF)
        r.gate[rr, :] = dmix.astype(BF)
        r.dn[rr, :] = dmix
        hi, lo = parts(dmix * r.care[rr, :].astype(F32), 2)
        r.sdm[rr, :] = hi
        r.care[rr, :] = lo
        r.cp[rr, :] = (dmix * r.cp[rr, :].astype(F32)).astype(BF)
        r.acc[0] = r.acc[0] + fold8(dn * scaled)
        r.acc[1] = r.acc[1] + fold8(dmix * val)

    rows_loop(tok, RT, body)

    r.run[...] = jnp.zeros((ns, w), F32)
    for c in range(nb - 1, -1, -1):
        rr = slice(c * L, (c + 1) * L)
        r.mixer[rr, :] = mm(r.stT[ns:s2, rr], r.sdm[rr, :]) + mm(r.stT[ns:s2, rr], r.care[rr, :])
        f = r.facr[8 * c : 8 * c + 1, :]

        def body(t, c=c, f=f):
            q = pl.ds(t, RT)
            r.run[q, :] = r.mixer[pl.ds(pl.multiple_of(c * L + t, RT), RT), :] + f * r.run[q, :]

        rows_loop(ns, RT, body)
    for k in range(1, p.reach + 1):

        @pl.when(ok_bwd(k, me))
        def _(k=k):
            fwd_copy(k).wait_send()

    send_states(bwd_copy, behind, lambda k: ok_fwd(k, me))

    for c in range(nb):
        rr = slice(c * L, (c + 1) * L)
        r.gtl[...] = (r.ends[c] - r.STb[c].astype(F32)).astype(BF)
        r.gBC[rr, ns:s2] = (
            mm_rt(r.sdm[rr, :], r.STb[c])
            + mm_rt(r.care[rr, :], r.STb[c])
            + mm_rt(r.sdm[rr, :], r.gtl[...])
        )
    r.rc[...] = mm_rt(r.cp[...], r.E[...])
    relay_states(bwd_copy, r.bin, behind, 1, 2)
    ar_service(0, 4)

    def weight_grad(lhs, rhs, into, width, step):
        def body(n):
            nn = pl.ds(n, step)
            full = mm(lhs[...], rhs[:, nn]).astype(BF)
            for k in range(dp):
                into[k, :, nn] = full[k * p.crow : (k + 1) * p.crow, :]

        rows_loop(width, step, body)

    weight_grad(r.tb, r.gn, r.g_out, w, nt)
    rs_send(p_out, 0)
    ar_service(4, 5)

    def transpose_nx():
        for c in range(nb):
            r.tb[:, c * L : (c + 1) * L] = r.nx[HALO + c * L : HALO + (c + 1) * L, :].T

    ar_service(5, 6)

    def within_back(c, carry):
        rr, b_rows, c_rows, scores = in_block(c)
        two = jnp.concatenate([scores, scores], axis=0)
        r.gsc[...] = jnp.zeros((L, L), F32)
        r.rs[...] = r.rc[rr, :]
        r.colT[...] = jnp.zeros((LANES, L), F32)
        low = lane_l < HEADDIM
        for pr in range(pairs):
            pc = slice(pr * LANES, (pr + 1) * LANES)
            dm = r.gate[rr, pc]
            zero = jnp.zeros_like(dm)
            stacked = jnp.concatenate([jnp.where(low, dm, zero), jnp.where(low, zero, dm)], axis=0)
            fine = r.dn[rr, pc] - dm.astype(F32)
            fine = jnp.concatenate([jnp.where(low, fine, 0.0), jnp.where(low, 0.0, fine)], axis=0).astype(BF)
            gm = mm_rt(stacked, r.wtd[rr, pc]) + mm_rt(fine, r.wtd[rr, pc])
            dec = r.D[c * pairs + pr].astype(F32)
            xx = gm * dec
            r.gsc[...] = r.gsc[...] + (xx[0:L] + xx[L:])
            mix = (dec * two).astype(BF)
            gap = (xx * two).astype(BF)
            gapf = gap.astype(F32)
            total = r.rs[...]
            for half in (0, 1):
                h = 2 * pr + half
                hot = jnp.where(lane_l == h, 1.0, 0.0).astype(BF)
                total = total + mm(gap[half * L : (half + 1) * L], hot)
                r.colT[h : h + 1, :] = jnp.sum(gapf[half * L : (half + 1) * L], axis=0, keepdims=True)
            r.rs[...] = total
            r.dn[rr, pc] = mm_lt(mix, stacked)
        low_scores = r.gsc[...].astype(BF)
        r.gBC[rr, ns:s2] = r.gBC[rr, ns:s2] + mm(low_scores, b_rows)
        r.gBC[rr, 0:ns] = mm_lt(low_scores, c_rows)
        r.rc[rr, :] = r.rs[...] - r.colT[...].T
        return carry

    lax.fori_loop(0, nb // 2, within_back, 0)
    rs_take(p_out, 0)
    ar_service(6, 8)
    lax.fori_loop(nb // 2, nb, within_back, 0)
    ar_service(8, 10)

    relay_states(bwd_copy, r.bin, behind, 2, p.group)
    transpose_nx()
    weight_grad(r.tb, r.dgate, r.g_gate, w, nt)
    rs_send(p_gate, 0)
    receive_states(bwd_copy, r.bin, behind, lambda k: ok_bwd(k, me))
    for c in range(nb - 1, -1, -1):
        rr = slice(c * L, (c + 1) * L)
        f = r.facr[8 * c : 8 * c + 1, :]
        r.gf[8 * c : 8 * c + 8, :] = jnp.zeros((8, w), F32)

        def body(t, c=c, f=f):
            q = pl.ds(t, RT)
            now = r.run[q, :]
            gf = r.gf[8 * c : 8 * c + 8, :]
            r.gf[8 * c : 8 * c + 8, :] = gf + fold8(now * r.ends[c, q, :])
            hi, lo = parts(now, 2)
            r.gtl[q, :] = lo
            r.STb[c, q, :] = hi
            r.run[q, :] = r.mixer[pl.ds(pl.multiple_of(c * L + t, RT), RT), :] + f * now

        rows_loop(ns, RT, body)
        gf = jnp.sum(r.gf[8 * c : 8 * c + 8, :], axis=0, keepdims=True) * f
        r.gf[8 * c : 8 * c + 8, :] = jnp.broadcast_to(gf, (8, w))
        r.mixer[rr, :] = mm(r.st[rr, 0:ns], r.STb[c])
        r.gBC[rr, 0:ns] = r.gBC[rr, 0:ns] + (
            mm_rt(r.tw[rr, :], r.STb[c]) + mm_rt(r.tw[rr, :], r.gtl[...])
        )

    def body(t):
        rr = pl.ds(t, RT)
        thr = r.mixer[rr, :]
        gw_ = r.dn[rr, :] + r.taile[rr, :].astype(F32) * thr
        val = r.val[rr, :].astype(F32)
        dval = skip_row * r.gate[rr, :].astype(F32) + gw_ * r.stepe[rr, :]
        r.sdm[rr, :] = (gw_ * val).astype(BF)
        r.cp[rr, :] = (r.tw[rr, :].astype(F32) * thr).astype(BF)
        r.dn[rr, :] = dval * r.vgr[rr, :].astype(F32)
        r.dsp[rr, :] = r.gBC[rr, :] * r.sgr[rr, :].astype(F32)

    rows_loop(tok, RT, body)

    def back_copy(which):
        buf = r.dn if which == 0 else r.dsp
        return remote(
            buf.at[pl.ds(0, 8), :], buf.at[pl.ds(tok, 8), :], r.halo_sem.at[2 + which], r.halo_sem.at[4 + which],
            DP, jnp.maximum(me - 1, 0),
        )

    @pl.when(has_prev)
    def _():
        back_copy(0).start()
        back_copy(1).start()

    @pl.when(jnp.logical_not(has_next))
    def _():
        r.dn[tok : tok + 8, :] = jnp.zeros((8, w), F32)
        r.dsp[tok : tok + 8, :] = jnp.zeros((8, s2), F32)

    ar_service(10, 12)
    rs_take(p_gate, 0)

    up = jnp.where(lane_l >= row_l, 1.0, 0.0).astype(BF)
    below = jnp.where(lane_l < row_l, 1.0, 0.0).astype(BF)
    r.sacc[...] = jnp.zeros((4, 8, LANES), F32)
    for c in range(nb):
        rr = slice(c * L, (c + 1) * L)
        direct = mm_rt(r.sdm[rr, :], r.E[...])
        tails = mm_rt(r.cp[rr, :], r.E[...])
        gf = mm_rt_fine(r.gf[8 * c : 8 * c + 8, :], r.E[...], 3)[0:1]
        q = mm_fine_right(up, r.rc[rr, :], 3) + mm_fine_right(below, tails, 3) + gf
        steps = r.steps[rr, :]
        dstep = decay_row * q + direct
        dpre = dstep * sigmoid(r.sp[rr, :])
        r.dst[rr, :] = dpre.astype(BF)
        r.sacc[0] = r.sacc[0] + fold8(dpre)
        r.sacc[1] = r.sacc[1] + fold8(q * steps * decay_row)


    @pl.when(has_next)
    def _():
        back_copy(0).wait_recv()
        back_copy(1).wait_recv()

    def unmasked(grads, at, back):
        return jnp.where(at >= back, grads, 0.0) if back and not p.aligned else grads

    def conv_back(dpre, cw, width, out, fine=None):
        def body(t):
            grads = dpre[pl.ds(t, RT + 8), :]
            at = None if p.aligned else place(t, RT + 8, width)
            total = jnp.zeros((RT, width), F32)
            for k in range(p.taps):
                back = p.taps - 1 - k
                total = total + cw[k : k + 1, :] * unmasked(grads, at, back)[back : back + RT]
            hi, lo = parts(total, 2)
            out[pl.ds(t, RT), :] = hi
            if fine is not None:
                fine[pl.ds(t, RT), :] = lo

        rows_loop(tok, RT, body)

    conv_back(r.dsp, r.scw, s2, r.st, r.dsl)
    conv_back(r.dn, r.cw, w, r.wtd)


    def keep_out(rr, total):
        r.w_out[rr, :] = total

    def keep_gate(rr, total):
        r.w_gate[rr, :] = total

    def keep_va(rr, total):
        r.w_value[rr, 0 : p.cut] = total

    def keep_vb(rr, total):
        r.w_value[rr, p.cut : w] = total

    def keep_ss(rr, total):
        r.sq[rr, :] = total[:, 0:s2].astype(BF)
        r.sc[rr, :] = total[:, s2 : s2 + LANES]

    ar_service(12, 15)
    rs_take(p_out, 1, keep_out)
    r.pacc[...] = jnp.zeros((8, d), F32)
    r.sc[...] = jnp.zeros((tok, LANES), F32)

    def in_tile(n):
        nn = pl.ds(n, 256)
        r.mixer[:, 0:256] = (
            mm_rt(r.dgate[...], r.gw[nn, :])
            + mm_rt(r.wtd[...], r.vw[nn, :])
            + mm_rt(r.st[...], r.sw[nn, :])
            + mm(r.dst[...], r.swp[:, nn])
        )

        def body(t, j):
            rr = pl.ds(pl.multiple_of(j * SUB + t, RT), RT)
            grad = r.mixer[rr, 0:256]
            gx = grad * r.x[rr, nn].astype(F32)
            r.pacc[:, nn] = r.pacc[:, nn] + fold8(gx * wide(r.invin[rr, :], 2))
            gx = gx * r.pg[0:1, nn]
            r.sc[rr, :] = r.sc[rr, :] + (gx[:, 0:LANES] + gx[:, LANES:])
            low_grad = grad.astype(BF)
            for half in range(2):
                r.D[(n // LANES + half) * nsub + j, pl.ds(t, RT), :] = low_grad[:, half * LANES : (half + 1) * LANES]

        for j in range(nsub):
            rows_loop(SUB, RT, functools.partial(body, j=j))

    rows_loop(d // 2, 256, in_tile)
    ar_service(15, 16)
    rows_loop(d // 2, 256, lambda n: in_tile(pl.multiple_of(n + d // 2, 256)))

    def body(t):
        rr = pl.ds(t, L)
        r.sc[rr, :] = jnp.broadcast_to(jnp.sum(r.sc[rr, :], axis=1, keepdims=True), (L, LANES))

    rows_loop(tok, L, body)
    zx_send(1, r.sc)
    ar_service(16, 19)

    zs, sm = r.zs, r.sm.at[0]
    quarter = d // 4
    sm[...] = jnp.zeros((16, w), F32)

    def conv_sums(raw, dpre, width):
        cacc = r.cacc
        cacc[:, :, 0:width] = jnp.zeros((p.taps + 1, 8, width), F32)

        def body(t):
            win = raw[pl.ds(t, RT + HALO), :].astype(F32)
            grads = dpre[pl.ds(t, RT), :]
            at = None if p.aligned else place(t, RT, width)
            cacc[p.taps, :, 0:width] = cacc[p.taps, :, 0:width] + fold8(grads)
            for k in range(p.taps):
                back = p.taps - 1 - k
                term = unmasked(grads, at, back) * win[HALO - back : HALO - back + RT]
                cacc[k, :, 0:width] = cacc[k, :, 0:width] + fold8(term)

        rows_loop(tok, RT, body)
        return [jnp.sum(cacc[k, :, 0:width], axis=0, keepdims=True) for k in range(p.taps + 1)]

    sums = conv_sums(r.sraw, r.dsp, s2)
    for k in range(p.taps):
        zs[rank, 4 + k : 5 + k, 0:s2] = sums[k]
    for k in range(2):
        zs[rank, 4 + k : 5 + k, s2 : s2 + LANES] = sums[p.taps][:, k * LANES : (k + 1) * LANES]
    zs[rank, 6:8, s2 : s2 + LANES] = jnp.zeros((2, LANES), F32)
    gains = jnp.sum(r.pacc[...], axis=0, keepdims=True)
    for k in range(4):
        zs[rank, k : k + 1, :] = gains[:, k * quarter : (k + 1) * quarter]
    for off in range(1, tp):
        slot_copy(r.zs, r.zssem, TP, rank, tp, off).start()

    ar_service(19, 20)
    zx_take(1, r.sc)

    def body(t):
        rr = pl.ds(t, L)
        inv = r.invin[rr, :]
        r.coefo[rr, :] = inv * inv * inv * (r.sc[rr, 0:1] * (1.0 / d))

    rows_loop(tok, L, body)
    ar_service(20, 21)
    give = [
        pltpu.make_async_copy(src, dst, r.osem.at[i])
        for i, (src, dst) in enumerate(((r.w_out, r.o_out), (r.w_gate, r.o_gate), (r.w_value, r.o_value)))
    ]
    for s in range(2, p.nbits):
        rs_take(p_out, s, keep_out)
    give[0].start()
    ar_service(21, 23)
    rs_take(p_gate, 1, keep_gate)
    rs_finish(p_out)
    weight_grad(r.tb, r.wtd, r.g_out, w, nt)
    rs_send(p_va, 0)
    rs_send(p_vb, 0)
    ar_service(23, 25)
    full = (mm(r.tb[...], r.st[...]) + mm(r.tb[...], r.dsl[...])).astype(BF)
    for k in range(dp):
        r.g_ss[k, :, 0:s2] = full[k * p.crow : (k + 1) * p.crow, :]
    full = mm(r.tb[...], r.dst[...]).astype(BF)
    for k in range(dp):
        r.g_ss[k, :, s2 : s2 + LANES] = full[k * p.crow : (k + 1) * p.crow, :]
    rs_send(p_ss, 0)

    for off in range(1, tp):
        slot_copy(r.zs, r.zssem, TP, rank, tp, off).wait_recv()
    total = zs[0]
    for k in range(1, tp):
        total = total + zs[k]
    sm[8:16, 0:quarter] = total
    sums = conv_sums(r.vraw, r.dn, w)
    for k in range(p.taps + 1):
        sm[k : k + 1, :] = sums[k]
    sm[5:6, :] = jnp.sum(r.acc[0], axis=0, keepdims=True)
    sm[6:7, 0:LANES] = jnp.sum(r.sacc[0], axis=0, keepdims=True)
    sm[6:7, LANES : 2 * LANES] = jnp.sum(r.sacc[1], axis=0, keepdims=True)
    sm[7:8, 0:LANES] = mm_rt_fine(
        jnp.broadcast_to(jnp.sum(r.acc[1], axis=0, keepdims=True), (8, w)), r.E[...], 3
    )[0:1]
    sm_copy(0).start()

    ar_service(25, 27)
    late = ((p_va, keep_va), (p_vb, keep_vb), (p_ss, keep_ss))
    sm_take(0)
    for piece, out in late:
        rs_take(piece, 0, out)
    ar_service(27, 31)
    for s in range(2, p.nbits):
        rs_take(p_gate, s, keep_gate)
    give[1].start()
    ar_service(31, 38)
    at = 38
    for s in range(1, p.nbits):
        sm_take(s)
        for piece, out in late:
            rs_take(piece, s, out)
        if s < p.nbits - 1:
            ar_service(at, at + 7)
            at += 7
    give[2].start()

    def sq_copy(src, dst, ssem, rsem, to):
        return remote(src, dst, r.sqsem.at[ssem], r.sqsem.at[rsem], TP, to)

    sq_in = lambda src: sq_copy(src, r.sq_in, 0, 1, inward)
    sq_swap = lambda: sq_copy(r.sq_in, r.sq_x, 0, 2, inward)
    sq_out = lambda: sq_copy(r.sq_x, r.sq_x, 3, 4, outward)

    def sq_rows(fn):
        rows_loop(p.crow, RT, lambda t: fn(pl.ds(t, RT)))

    @pl.when(end)
    def _():
        sq_in(r.sq).start()

    ar_service(at, at + 2)

    @pl.when(jnp.logical_not(end))
    def _():
        sq_in(r.sq).wait_recv()

        def body(rr):
            r.sq_in[rr, :] = (r.sq_in[rr, :].astype(F32) + r.sq[rr, :].astype(F32)).astype(BF)

        sq_rows(body)
        if half_t > 2:

            @pl.when(jnp.logical_not(mid))
            def _():
                sq_in(r.sq_in).start()

        @pl.when(mid)
        def _():
            sq_swap().start()

    ar_service(at + 2, at + 4)
    at += 4

    @pl.when(mid)
    def _():
        sq_swap().wait()

        def body(rr):
            r.sq_x[rr, :] = (r.sq_in[rr, :].astype(F32) + r.sq_x[rr, :].astype(F32)).astype(BF)

        sq_rows(body)
        sq_out().start()


    for c in range(-(-p.crow // LANES)):
        width = min(LANES, p.crow - c * LANES)
        r.o_step[:, c * LANES : c * LANES + width] = r.sc[c * LANES : (c + 1) * LANES, :].T[0 : p.h, 0:width]

    total = r.sm[p.nbits]
    r.o_cw[...] = total[0 : p.taps]
    r.o_cb[...] = total[p.taps : p.taps + 1]
    r.o_ng[...] = total[5:6]
    r.o_sb[...] = total[6:7, 0 : p.h]
    r.o_dl[...] = total[6:7, LANES : LANES + p.h]
    r.o_sk[...] = total[7:8, 0 : p.h]
    r.o_scw[...] = total[12 : 12 + p.taps, 0:s2]
    for k in range(2):
        r.o_scb[:, k * LANES : (k + 1) * LANES] = total[12 + k : 13 + k, s2 : s2 + LANES]
    own = jnp.zeros((1, p.crow), F32)
    per = quarter // p.crow
    for k in range(dp):
        piece = total[8 + k // per : 9 + k // per, k % per * p.crow : (k % per + 1) * p.crow]
        own = own + jnp.where(me == k, piece, 0.0)
    r.o_pg[...] = own

    for c in few_gives[1:]:
        c.start()
    ar_service(at, last_step)

    @pl.when(jnp.logical_not(mid))
    def _():
        sq_in(r.sq).wait_send()
        sq_out().wait_recv()
        if half_t > 2:

            @pl.when(jnp.logical_not(end))
            def _():
                sq_out().start()

    @pl.when(jnp.logical_not(end))
    def _():
        sq_out().wait_send()

    def body(rr):
        r.o_state[rr, :] = r.sq_x[rr, :].astype(F32)

    sq_rows(body)
    few_gives[0].start()

    for s in range(last_step - FIN, 2 * nch):
        ar_finish(*divmod(s, nch))
    for s in range(last_step - KEPT, 2 * nch):
        ar_kept(*divmod(s, nch))
    for c in give + few_gives:
        c.wait()
    for piece in (p_gate, p_va, p_vb, p_ss):
        rs_finish(piece)
    for off in range(1, tp):
        zx_copy(0, off).wait_send()
        zx_copy(1, off).wait_send()
        slot_copy(r.zs, r.zssem, TP, rank, tp, off).wait_send()
    for s in range(p.nbits):
        sm_copy(s).wait_send()

    @pl.when(has_next)
    def _():
        halo_copy().wait_send()

    @pl.when(has_prev)
    def _():
        back_copy(0).wait_send()
        back_copy(1).wait_send()

    for k in range(1, p.reach + 1):

        @pl.when(ok_fwd(k, me))
        def _(k=k):
            bwd_copy(k).wait_send()


def on_device(
    mesh, x, lens, pg, gw, vw, sw, stepw, cw, cb, scw, scb, sb, dl, sk, ng, ow, og
):
    row = lambda a: a.reshape(1, -1)
    big = (x, gw, vw, sw, ow, og)
    small = dict(
        pg_in=pg, stepw=stepw.T, cw=cw, cb_in=cb, scw=scw, scb=row(scb), sb=row(sb), dl=row(dl),
        sk=row(sk), ng_in=ng,
    )
    p = Plan(mesh, x, lens, gw, sw, stepw.T, cw)
    scratch = scratch_of(p)
    for k, v in small.items():
        scratch[k] = pltpu.VMEM(v.shape, v.dtype)
    f = lambda *s: jax.ShapeDtypeStruct(s, F32)
    rows = jax.ShapeDtypeStruct((p.tok, p.d), BF)
    shapes = dict(
        o_block=rows, o_input=rows, o_pg=f(1, p.crow), o_gate=f(p.crow, p.w), o_value=f(p.crow, p.w),
        o_state=f(p.crow, p.s2), o_step=f(p.h, p.crow), o_cw=f(p.taps, p.w), o_cb=f(1, p.w),
        o_scw=f(p.taps, p.s2), o_scb=f(1, p.s2), o_sb=f(1, p.h), o_dl=f(1, p.h), o_sk=f(1, p.h),
        o_ng=f(1, p.w), o_out=f(p.crow, p.w),
    )
    few_out = tuple(reversed([k for k in shapes if k not in BY_COPY and k != STATE_OUT])) + (STATE_OUT,)
    few_out = few_out[::-1]
    for k in few_out:
        scratch[k] = pltpu.VMEM(shapes[k].shape, F32)
    scratch[FEW_SEM] = pltpu.SemaphoreType.DMA((2, max(len(small), len(few_out))))
    any_ = pl.BlockSpec(memory_space=pl.ANY)
    smem = pl.BlockSpec(memory_space=pltpu.SMEM)
    unnamed = tuple("s" + str(i) for i in range(len(big)))
    hbm = lambda keys: tuple(HBM + k if k in scratch else k for k in keys)
    names = unnamed + ("lens",) + hbm(small) + hbm(shapes) + tuple(scratch)
    outs = pl.pallas_call(
        functools.partial(kernel, p, names, tuple(small), few_out),
        out_shape=tuple(shapes.values()),
        in_specs=[any_] * len(big) + [smem] + [any_] * len(small),
        out_specs=[any_] * len(shapes),
        scratch_shapes=list(scratch.values()),
        compiler_params=pltpu.CompilerParams(
            collective_id=0, has_side_effects=True, vmem_limit_bytes=VMEM_BYTES
        ),
    )(*big, lens, *small.values())
    outs = deliver(outs)
    names = list(shapes)
    turned = (names.index(STEP_OUT), names.index(OUT_OUT))
    return tuple(o.T if i in turned else o for i, o in enumerate(outs))


STEP_OUT, OUT_OUT, STATE_OUT = "o_step", "o_out", "o_state"
HBM, FEW_SEM = "hbm_", "few_sem"
BY_COPY = ("o_block", "o_input", "o_gate", "o_value", "o_out")


def deliver(outs):
    count = len(outs)
    flat = [o.shape[0] == 1 for o in outs]
    shapes = [jax.ShapeDtypeStruct(o.shape[1:] if f else o.shape, o.dtype) for o, f in zip(outs, flat)]

    def body(*refs):
        ins, res, sems = refs[:count], refs[count : 2 * count], refs[2 * count]
        here = refs[2 * count + 1 : 3 * count + 1]
        rows = dict(zip([i for i in range(count) if flat[i]], refs[3 * count + 1 :]))
        reads = [pltpu.make_async_copy(ins[i], here[i], sems.at[0, i]) for i in range(count)]
        writes = [pltpu.make_async_copy(rows.get(i, here[i]), res[i], sems.at[1, i]) for i in range(count)]
        for c in reads:
            c.start()
        for i in range(count):
            reads[i].wait()
            if flat[i]:
                rows[i][...] = here[i][...].reshape(rows[i].shape)
            writes[i].start()
        for c in writes:
            c.wait()

    any_ = pl.BlockSpec(memory_space=pl.ANY)
    return pl.pallas_call(
        body,
        out_shape=shapes,
        in_specs=[any_] * count,
        out_specs=[any_] * count,
        scratch_shapes=[pltpu.SemaphoreType.DMA((2, count))]
        + [pltpu.VMEM(o.shape, o.dtype) for o in outs]
        + [pltpu.VMEM(s.shape, s.dtype) for s, f in zip(shapes, flat) if f],
        compiler_params=pltpu.CompilerParams(vmem_limit_bytes=VMEM_BYTES),
    )(*outs)


def solution(mesh):
    t = TP
    in_specs = (
        P(DP, None), P(), P(), P(None, t), P(None, t), P(), P(None, t), P(None, t), P(t), P(), P(),
        P(t), P(t), P(t), P(t), P(t, None), P(DP, None),
    )
    out_specs = (
        P(DP, None), P(DP, None), P(DP), P(DP, t), P(DP, t), P(DP, None), P(DP, t),
        P(None, t), P(t), P(), P(), P(t), P(t), P(t), P(t), P(t, DP),
    )
    return jax.shard_map(
        functools.partial(on_device, mesh), mesh=mesh, in_specs=in_specs, out_specs=out_specs, check_vma=False
    )
```
